32 devices in a mesh: band: 4 (over y, core), slab: 8 (over z, x).
Axes of the slice: x: 2, y: 2, z: 4, core: 2. Of those that a mesh axis runs over, the one named last changes fastest.
Arguments:
- bands: float32 [8, 192, 192, 192], P('band', 'slab'), may hold values from -8 to 8
- occupied: float32 [16, 192, 192, 192], P('band', 'slab'), may hold values from -8 to 8
- occ_index: int32 [2], replicated, may hold values from 0 to 15
- band_pick: int32 [8], P('band'), may hold values from 0 to 1
Outputs:
- exchange_out: float32 [8, 192, 192, 192], P('band', 'slab')
The draws below stay inside these ranges and needn't reach their ends.
All inputs are finite; a program needn't handle non-finite values.
Results may differ from the reference program's by a relative error of at most 0.0001.
Values sent between devices are 32-bit elements; how exact they have to be, the bound alone decides.
No kernel may reach another device: no remote copies, remote signals or barrier semaphores. Data moves between devices by JAX's collectives and lax.ppermute only.
A program may use at most 192 MiB of HBM per device.

```python
import math
import jax
import jax.numpy as jnp
from jax import lax

NG = 192
BAND_DEV = 2
PAIR = 2
WIN = 2
BANDS = 8
OCC_ALL = 16
PICKS = 8


def orbital_values(key, count):
    shape = (count, NG, NG, NG)
    base = jnp.clip(jax.random.normal(key, shape, jnp.float32), -6.0, 6.0)
    return base


def draw_bands(key, part):
    return orbital_values(jax.random.fold_in(key, 11), BANDS)


def draw_occupied(key, part):
    return orbital_values(jax.random.fold_in(key, 23), OCC_ALL)


def place_ends(drawn, rng, low, high):
    longest = drawn.shape.index(max(drawn.shape))
    spots = []
    for shift in (0, 1):
        where = [jax.random.randint(jax.random.fold_in(rng, axis), (), 0, length) for axis, length in enumerate(drawn.shape)]
        where[longest] = (where[longest] + shift) % drawn.shape[longest]
        spots.append(tuple(where))
    return drawn.at[spots[0]].set(low).at[spots[1]].set(high)


def setup_inputs(seed: int = 0) -> dict:
    key_list = jax.random.split(jax.random.key(seed), 5)
    bands = draw_bands(jax.random.fold_in(key_list[4], 71), 0)
    occupied = draw_occupied(jax.random.fold_in(key_list[4], 71), 0)
    occ_index = jax.random.randint(key_list[2], (WIN,), 0, OCC_ALL).astype(jnp.int32)
    band_pick = place_ends(jax.random.randint(key_list[3], (PICKS,), 0, BAND_DEV), jax.random.fold_in(key_list[3], 1), 0, BAND_DEV - 1).astype(jnp.int32)
    return {"bands": bands, "occupied": occupied, "occ_index": occ_index, "band_pick": band_pick}


grid_step = 0.25
omega = 0.106


def wave_squared(length):
    modes = jnp.arange(length, dtype=jnp.int32)
    signed = jnp.where(modes <= length // 2, modes, modes - length)
    wave = (2.0 * math.pi / (length * grid_step)) * signed.astype(jnp.float32)
    return wave * wave


def screened(squares):
    nonzero = jnp.where(squares > 0, squares, jnp.ones_like(squares))
    value = 4.0 * math.pi * (1.0 - jnp.exp(-squares / (4.0 * omega * omega))) / nonzero
    return jnp.where(squares > 0, value, jnp.full_like(squares, math.pi / (omega * omega)))


def reference(bands, occupied, occ_index, band_pick):
    squares = wave_squared(NG)
    half_wave = squares[: NG // 2 + 1]
    kernel = screened(squares[:, None, None] + squares[None, :, None] + half_wave[None, None, :])
    rows = (jnp.arange(PICKS, dtype=jnp.int32) // PAIR) * BAND_DEV + band_pick.astype(jnp.int32)

    def one_row(row):
        target = lax.dynamic_index_in_dim(bands, row, 0, keepdims=False)

        def add_term(turn, total):
            which = occ_index[turn].astype(jnp.int32)
            orbital = lax.dynamic_index_in_dim(occupied, which, 0, keepdims=False)
            spectrum = jnp.fft.rfftn(orbital * target)
            potential = jnp.fft.irfftn(kernel * spectrum, s=(NG, NG, NG))
            return total - potential.astype(total.dtype) * orbital

        return lax.fori_loop(0, WIN, add_term, jnp.zeros((NG, NG, NG), bands.dtype))

    return lax.map(one_row, rows)
```

```python
import math

import jax
import jax.numpy as jnp
from jax import lax
from jax.experimental import pallas as pl
from jax.experimental.pallas import tpu as pltpu
from jax.sharding import PartitionSpec as P

grid_step = 0.25
omega = 0.106
CORES = 2
LANES = 128
STEP = 4
SPLIT = (3, 3, 3, 3)
HALVES = ((0, 1), (2, 3))
VMEM_LIMIT = 56 * 1024 * 1024


def wave_squared(modes, length):
    signed = jnp.where(modes <= length // 2, modes, modes - length)
    wave = 2.0 * math.pi / (length * grid_step) * signed.astype(jnp.float32)
    return wave * wave


def screened(squares):
    nonzero = jnp.where(squares > 0, squares, jnp.ones_like(squares))
    value = 4.0 * math.pi * (1.0 - jnp.exp(-squares / (4.0 * omega * omega))) / nonzero
    return jnp.where(squares > 0, value, jnp.full_like(squares, math.pi / (omega * omega)))


def cas_matrix(rows, columns, length):
    product = rows[:, None] * columns[None, :] % length
    phases = 2.0 * math.pi / length * product.astype(jnp.float32)
    return jnp.cos(phases) + jnp.sin(phases)


def halves(values):
    high = values.astype(jnp.bfloat16)
    low = (values - high.astype(jnp.float32)).astype(jnp.bfloat16)
    return high, low


def multiply(left, right):
    def dot(a, b):
        return jnp.dot(a, b, preferred_element_type=jnp.float32)

    return dot(left[0], right[0]) + (dot(left[0], right[1]) + dot(left[1], right[0]))


def pack_body(scalars, keep_ref, give_ref, keep_out, give_out):
    for source, out in ((keep_ref, keep_out), (give_ref, give_out)):
        rows = jnp.swapaxes(source[0], 0, 1)
        out[0, 0, 0] = rows[:STEP, :, :LANES]
        out[0, 0, 1] = rows[STEP:, :, :LANES]
        out[0, 0, 2] = jnp.concatenate([rows[:STEP, :, LANES:], rows[STEP:, :, LANES:]], axis=-1)


def pack(stored, scalars, units):
    count = scalars.shape[0] - 2
    planes, points = stored.shape[1], stored.shape[3]
    block = (1, 1, 3, STEP, planes, LANES)
    shape = jax.ShapeDtypeStruct((count, units) + block[2:], jnp.float32)
    spec = pl.BlockSpec(block, lambda i, u, s: (i, u, 0, 0, 0, 0))
    return pl.pallas_call(
        pack_body,
        grid_spec=pltpu.PrefetchScalarGridSpec(
            num_scalar_prefetch=1,
            grid=(count, units),
            in_specs=[
                pl.BlockSpec((1, planes, 2 * STEP, points), lambda i, u, s: (s[i], 0, s[count] + u, 0)),
                pl.BlockSpec((1, planes, 2 * STEP, points), lambda i, u, s: (s[i], 0, s[count + 1] + u, 0)),
            ],
            out_specs=[spec, spec],
        ),
        out_shape=[shape, shape],
        compiler_params=pltpu.CompilerParams(vmem_limit_bytes=VMEM_LIMIT),
        name="pack",
    )(scalars, stored, stored)


def unpack_body(scalars, keep_ref, got_ref, *rest):
    out = rest[-1]

    def place(source):
        lower = jnp.concatenate([source[0, 0, 0], source[0, 0, 2][:, :, : LANES // 2]], axis=-1)
        upper = jnp.concatenate([source[0, 0, 1], source[0, 0, 2][:, :, LANES // 2 :]], axis=-1)
        out[0] = jnp.swapaxes(jnp.concatenate([lower, upper], axis=0), 0, 1)

    pl.when(pl.program_id(1) == 0)(lambda: place(keep_ref))
    pl.when(pl.program_id(1) == 1)(lambda: place(got_ref))


def unpack(keep, got, scalars, shape, earlier):
    count, units = keep.shape[:2]
    planes, points = shape[1], shape[3]
    block = (1, 1, 3, STEP, planes, LANES)
    kept = pl.BlockSpec(block, lambda i, k, u, s: (i, jnp.where(k == 0, u, units - 1), 0, 0, 0, 0))
    other = pl.BlockSpec(block, lambda i, k, u, s: (i, jnp.where(k == 0, 0, u), 0, 0, 0, 0))
    held = [] if earlier is None else [earlier]
    return pl.pallas_call(
        unpack_body,
        grid_spec=pltpu.PrefetchScalarGridSpec(
            num_scalar_prefetch=1,
            grid=(count, 2, units),
            in_specs=[kept, other] + [pl.BlockSpec(memory_space=pl.ANY) for _ in held],
            out_specs=pl.BlockSpec(
                (1, planes, 2 * STEP, points), lambda i, k, u, s: (s[i], 0, s[count + k] + u, 0)
            ),
        ),
        out_shape=jax.ShapeDtypeStruct(shape, jnp.float32),
        input_output_aliases={3: 0} if held else {},
        compiler_params=pltpu.CompilerParams(vmem_limit_bytes=VMEM_LIMIT),
        name="unpack",
    )(scalars, keep, got, *held)


def orbital_parts(same, first, second):
    pieces = range(first.shape[0])
    near = [jnp.where(same, first[d, 0], second[d, 0]) for d in pieces]
    far = [jnp.where(same, second[d, 0], first[d, 0]) for d in pieces]
    return near + far


def forward_body(scalars, near, far, first, second, lower_ref, upper_ref, planes_ref, keep_out, give_out):
    orbitals = orbital_parts(scalars[0] == 1, first, second)
    targets = [part[d, 0] for part in (near, far) for d in range(part.shape[0])]
    density = jnp.concatenate([t * o for t, o in zip(targets, orbitals)], axis=2)
    step, points = density.shape[1], density.shape[2]
    matrix = halves(planes_ref[...])
    results = []
    for part, weights in ((0, lower_ref), (1, upper_ref)):
        packed = jnp.concatenate([density[part], density[2]], axis=-1).reshape(step * points, 2 * LANES)
        lines = multiply(halves(packed), halves(weights[...]))
        high, low = halves(lines)
        for row in range(step):
            where = slice(row * points, (row + 1) * points)
            results.append(multiply(matrix, (high[where], low[where])))
    spectrum = jnp.swapaxes(jnp.stack(results), 0, 1)
    keep_out[...] = spectrum[: points // 2]
    give_out[...] = spectrum[points // 2 :]


def stacked(array, offset):
    return pl.BlockSpec((array.shape[0], 1) + array.shape[2:], lambda u, s: (0, u + offset, 0, 0, 0, 0))


def forward(near, far, first, second, offset, scalars, lower, upper, planes_matrix):
    units, points = near.shape[1], planes_matrix.shape[0]
    whole = lambda a: pl.BlockSpec(a.shape, lambda u, s: (0, 0))
    out = pl.BlockSpec((points // 2, 2 * STEP, points), lambda u, s: (0, u, 0))
    shape = jax.ShapeDtypeStruct((points // 2, 2 * STEP * units, points), jnp.float32)
    return pl.pallas_call(
        forward_body,
        grid_spec=pltpu.PrefetchScalarGridSpec(
            num_scalar_prefetch=1,
            grid=(units,),
            in_specs=[stacked(near, 0), stacked(far, 0), stacked(first, offset), stacked(second, offset)]
            + [whole(lower), whole(upper), whole(planes_matrix)],
            out_specs=[out, out],
        ),
        out_shape=[shape, shape],
        compiler_params=pltpu.CompilerParams(vmem_limit_bytes=VMEM_LIMIT),
        name="forward",
    )(scalars, near, far, first, second, lower, upper, planes_matrix)


def middle_body(count, kernel_ref, forth_ref, back_ref, *refs):
    ins, outs = refs[:count], refs[count:]
    forth, back = halves(forth_ref[...]), halves(back_ref[...])
    for k in range(kernel_ref.shape[0]):
        rows = jnp.concatenate([r[k] for r in ins], axis=0)
        spectrum = multiply(forth, halves(rows)) * kernel_ref[k]
        filtered = multiply(back, halves(spectrum))
        start = 0
        for out in outs:
            out[k] = filtered[start : start + out.shape[1]]
            start += out.shape[1]


def middle(spectra, kernel, forth, back):
    count = len(spectra)
    deep, _, points = spectra[0].shape
    block = 4
    parts = [pl.BlockSpec((block,) + a.shape[1:], lambda k: (k, 0, 0)) for a in spectra]
    whole = pl.BlockSpec((points, points), lambda k: (0, 0))
    return pl.pallas_call(
        lambda *refs: middle_body(count, *refs),
        grid=(deep // block,),
        in_specs=[pl.BlockSpec((block, points, points), lambda k: (k, 0, 0)), whole, whole] + parts,
        out_specs=parts,
        out_shape=[jax.ShapeDtypeStruct(a.shape, jnp.float32) for a in spectra],
        compiler_params=pltpu.CompilerParams(vmem_limit_bytes=VMEM_LIMIT),
        name="middle",
    )(kernel, forth, back, *spectra)


def inverse_body(scalars, keep_ref, got_ref, first, second, lower_ref, upper_ref, planes_ref, near, far):
    spectrum = jnp.swapaxes(jnp.concatenate([keep_ref[...], got_ref[...]], axis=0), 0, 1)
    points = spectrum.shape[1]
    step = spectrum.shape[0] // 2
    matrix = halves(planes_ref[...])
    packed = []
    for part, weights in ((0, lower_ref), (1, upper_ref)):
        lines = jnp.concatenate(
            [multiply(matrix, halves(spectrum[part * step + row])) for row in range(step)], axis=0
        )
        packed.append(multiply(halves(lines), halves(weights[...])).reshape(step, points, 2 * LANES))
    low, high = packed
    field = [low[:, :, :LANES], high[:, :, :LANES], low[:, :, LANES:] + high[:, :, LANES:]]
    orbitals = orbital_parts(scalars[0] == 1, first, second)
    outs = [(part, d) for part in (near, far) for d in range(part.shape[0])]
    planes = points // len(outs)
    for i, (orbital, (out, d)) in enumerate(zip(orbitals, outs)):
        for part in range(3):
            out[d, 0, part] = -field[part][:, i * planes : (i + 1) * planes] * orbital[part]


def inverse(keep, got, first, second, offset, scalars, lower, upper, planes_matrix):
    deep, rows, points = keep.shape
    units = rows // (2 * STEP)
    whole = lambda a: pl.BlockSpec(a.shape, lambda u, s: (0, 0))
    part = pl.BlockSpec((deep, 2 * STEP, points), lambda u, s: (0, u, 0))
    shape = jax.ShapeDtypeStruct(first.shape[:1] + (units,) + first.shape[2:], jnp.float32)
    return pl.pallas_call(
        inverse_body,
        grid_spec=pltpu.PrefetchScalarGridSpec(
            num_scalar_prefetch=1,
            grid=(units,),
            in_specs=[part, part, stacked(first, offset), stacked(second, offset)]
            + [whole(lower), whole(upper), whole(planes_matrix)],
            out_specs=[stacked(shape, 0)] * 2,
        ),
        out_shape=[shape] * 2,
        compiler_params=pltpu.CompilerParams(vmem_limit_bytes=VMEM_LIMIT),
        name="inverse",
    )(scalars, keep, got, first, second, lower, upper, planes_matrix)


def by_layers(bands, occupied, occ_index, band_pick, groups, slabs):
    picks, window = band_pick.shape[0], occ_index.shape[0]
    per_group, planes, points = occupied.shape[0], bands.shape[1], bands.shape[2]
    sides = window
    layers = slabs // sides
    half_rows = points // CORES
    units = half_rows // (2 * STEP)
    chunks = len(SPLIT)
    starts = [sum(SPLIT[:j]) for j in range(chunks)]

    band, slab = lax.axis_index("band"), lax.axis_index("slab")
    y, c = band // CORES, band % CORES
    z, x = slab // sides, slab % sides

    def swap(values, axis, size, flip):
        return lax.ppermute(values, axis, [(i, flip(i)) for i in range(size)])

    def over_core(values):
        return swap(values, "band", groups, lambda i: i ^ 1)

    def over_y(values):
        return swap(values, "band", groups, lambda i: i ^ CORES)

    def over_x(values):
        return swap(values, "slab", slabs, lambda i: i ^ 1)

    def over_z(values, d):
        return swap(values, "slab", slabs, lambda i: i ^ (d * sides))

    layer_of = z ^ jnp.arange(layers, dtype=jnp.int32)
    side_of = x ^ jnp.arange(sides, dtype=jnp.int32)
    slab_of = (side_of[:, None] + sides * layer_of[None, :]).reshape(-1)
    plane_of = (slab_of[:, None] * planes + jnp.arange(planes, dtype=jnp.int32)).reshape(-1)
    core_of = c ^ jnp.arange(CORES, dtype=jnp.int32)
    all_modes = jnp.arange(points, dtype=jnp.int32)
    mode_of = (core_of[:, None] * half_rows + jnp.arange(half_rows, dtype=jnp.int32)).reshape(-1)

    columns = cas_matrix(all_modes, all_modes, points)
    empty = jnp.zeros((points - LANES, points), jnp.float32)
    lower = jnp.concatenate([columns, empty], axis=0)
    upper = jnp.concatenate([columns[:LANES], empty, columns[LANES:]], axis=0)
    lower_back = jnp.concatenate([columns, empty.T], axis=1)
    upper_back = jnp.concatenate([columns[:, :LANES], empty.T, columns[:, LANES:]], axis=1)
    to_modes = cas_matrix(mode_of, plane_of, points)
    to_planes = cas_matrix(plane_of, mode_of, points)
    forth = cas_matrix(all_modes, mode_of, points)
    back = cas_matrix(mode_of, all_modes, points)
    squares = wave_squared(all_modes, points)
    own_squares = wave_squared(c * half_rows + jnp.arange(half_rows, dtype=jnp.int32), points)
    kernel = screened(own_squares[:, None, None] + squares[None, :, None] + squares[None, None, :])
    kernel = kernel / float(points * points * points)

    first_bit = z % picks
    target_index = band_pick[jnp.arange(picks, dtype=jnp.int32) ^ first_bit]
    which = occ_index[side_of]
    owner = which // per_group
    owner_y, owner_core = owner // CORES, owner % CORES
    here = z // picks == c
    same = x == y
    flag = same.astype(jnp.int32)[None]

    def row_blocks(start):
        return jnp.stack([c * units + start, (1 - c) * units + start])

    def sync(*values):
        return lax.optimization_barrier(values)

    def pack_orbital(h):
        chosen = HALVES[h]
        size = sum(SPLIT[j] for j in chosen)
        return pack(occupied, jnp.concatenate([which % per_group, row_blocks(starts[chosen[0]])]), size)

    def pack_target(j):
        return pack(bands, jnp.concatenate([target_index, row_blocks(starts[j])]), SPLIT[j])

    def prepare_orbital(keep, got):
        mine = jnp.where(owner_core[0] == c, keep[0], got[0])
        theirs = jnp.where(owner_core[1] == c, keep[1], got[1])
        other = over_x(theirs)
        send = jnp.where(same, other, mine)
        stay = jnp.where(same, mine, other)
        return jnp.where(owner_y[0] == y, stay, over_y(send))

    def choose_targets(keep, got):
        pieces = []
        for d in range(layers):
            a, b = (keep, got) if d < picks else (got, keep)
            pieces.append(jnp.where(here, a[d % picks], b[d % picks]))
        return pieces

    def along_layers(pieces, carried):
        got, reached, size = [], [], pieces[0].shape[0]
        for d, piece in enumerate(pieces):
            if d == 0:
                got.append(piece)
                reached.append(carried)
            elif carried is None:
                got.append(over_z(piece, d))
            elif d & (d - 1):
                reach = d & -d
                got.append(over_z(piece, d))
                reached.append(over_z(reached[d - reach], reach))
            else:
                both = over_z(jnp.concatenate([piece, carried], axis=0), d)
                got.append(both[:size])
                reached.append(both[size:])
        return jnp.stack(got), None if carried is None else jnp.stack(reached)

    constants = sync(kernel, lower, upper, to_modes, to_planes, forth, back, lower_back, upper_back)
    orbital_give, target_give = {}, {}
    orbital_keep, orbital_got, target_keep, target_got = {}, {}, {}, {}
    orbital_keep[0], orbital_give[0] = pack_orbital(0)
    target_keep[0], target_give[0] = pack_target(0)
    orbital_got[0] = over_core(orbital_give[0])
    target_got[0] = over_core(target_give[0])
    orbital_keep[1], orbital_give[1] = pack_orbital(1)
    target_keep[1], target_give[1] = pack_target(1)
    orbital_got[0], target_got[0], orbital_give[1], target_give[1] = sync(
        orbital_got[0], target_got[0], orbital_give[1], target_give[1]
    )
    carried0 = prepare_orbital(orbital_keep[0], orbital_got[0])
    near0, _ = along_layers(choose_targets(target_keep[0], target_got[0]), None)
    orbital_got[1] = over_core(orbital_give[1])
    target_got[1] = over_core(target_give[1])
    target_keep[2], target_give[2] = pack_target(2)
    carried0, near0, orbital_got[1], target_got[1], target_give[2], constants = sync(
        carried0, near0, orbital_got[1], target_got[1], target_give[2], constants
    )
    kernel, lower, upper, to_modes, to_planes, forth, back, lower_back, upper_back = constants
    near1, first0 = along_layers(choose_targets(target_keep[1], target_got[1]), carried0)
    far0 = over_x(near0)
    carried1 = prepare_orbital(orbital_keep[1], orbital_got[1])
    target_got[2] = over_core(target_give[2])
    target_keep[3], target_give[3] = pack_target(3)
    near1, first0, far0, carried1, target_got[2], target_give[3] = sync(
        near1, first0, far0, carried1, target_got[2], target_give[3]
    )
    near2, first1 = along_layers(choose_targets(target_keep[2], target_got[2]), carried1)
    far1 = over_x(near1)
    second0 = over_y(first0)
    target_got[3] = over_core(target_give[3])
    near2, first1, far1, second0, target_got[3] = sync(near2, first1, far1, second0, target_got[3])
    near3, _ = along_layers(choose_targets(target_keep[3], target_got[3]), None)
    far2 = over_x(near2)
    second1 = over_y(first1)
    keep0, give0 = forward(near0, far0, first0, second0, 0, flag, lower, upper, to_modes)
    near3, far2, keep0, give0 = sync(near3, far2, keep0, give0)
    far3 = over_x(near3)
    spectra_got = {0: over_core(give0)}
    keep1, give1 = forward(near1, far1, first0, second0, SPLIT[0], flag, lower, upper, to_modes)
    spectra_got[1] = over_core(give1)
    keep2, give2 = forward(near2, far2, first1, second1, 0, flag, lower, upper, to_modes)
    spectra_got[2] = over_core(give2)
    keep3, give3 = forward(near3, far3, first1, second1, SPLIT[2], flag, lower, upper, to_modes)
    spectra_got[3] = over_core(give3)

    order = range(chunks)
    filtered = middle([keep0, keep1, keep2, keep3] + [spectra_got[j] for j in order], kernel, forth, back)

    orbit = [(first0, second0, 0), (first0, second0, SPLIT[0]), (first1, second1, 0), (first1, second1, SPLIT[2])]
    result = None
    queue = list(reversed(order))
    back_got = {j: over_core(filtered[chunks + j]) for j in queue}
    fields, home = {}, {}
    for turn in range(chunks + 2):
        if turn < chunks:
            j = queue[turn]
            fields[j] = inverse(filtered[j], back_got[j], *orbit[j], flag, lower_back, upper_back, to_planes)
        if turn:
            fields, home, result = sync(fields, home, result)
            fields, home = dict(fields), dict(home)
        if turn < chunks:
            near, far = fields[j]
            fields[j] = near, over_x(far)
        if 0 <= turn - 1 < chunks:
            j = queue[turn - 1]
            near, got = fields.pop(j)
            home[j] = [near[d] + got[d] for d in range(layers)]
            home[j] = [piece if d == 0 else over_z(piece, d) for d, piece in enumerate(home[j])]
        if 0 <= turn - 2:
            j = queue[turn - 2]
            pieces = home.pop(j)
            near, far = jnp.stack(pieces[:picks]), jnp.stack(pieces[picks:])
            keep = jnp.where(here, near, far)
            got = over_core(jnp.where(here, far, near))
            index = jnp.arange(picks, dtype=jnp.int32) ^ first_bit
            shape = (picks,) + bands.shape[1:]
            result = unpack(keep, got, jnp.concatenate([index, row_blocks(starts[j])]), shape, result)
    return result


def broadcast(x, axis, root):
    mine = lax.axis_index(axis) == root
    return lax.psum(jnp.where(mine, x, jnp.zeros_like(x)), axis)


def by_lines(bands, occupied, occ_index, band_pick):
    points, planes = bands.shape[2], bands.shape[1]
    window, per_group = occ_index.shape[0], occupied.shape[0]
    modes = jnp.arange(points, dtype=jnp.int32)
    matrix = cas_matrix(modes, modes, points)
    squares = wave_squared(modes, points)

    def transform(pattern, values):
        return jnp.einsum(pattern, values, matrix, precision=lax.Precision.HIGHEST)

    along_z, along_y, along_x = "pxyz,zk->pxyk", "pxyz,yk->pxkz", "pxyz,xk->pkyz"
    offset = lax.axis_index("slab") * planes
    row_squares = lax.dynamic_slice_in_dim(squares, offset, planes)
    kernel = screened(squares[:, None, None] + row_squares[None, :, None] + squares[None, None, :])
    kernel = kernel / float(points * points * points)
    targets = jnp.take(bands, band_pick, axis=0)

    def fetch_orbital(turn):
        which = occ_index[turn]
        own_orbital = lax.dynamic_index_in_dim(occupied, which % per_group, 0, keepdims=False)
        return broadcast(own_orbital, "band", which // per_group)

    orbitals = lax.map(fetch_orbital, jnp.arange(window, dtype=jnp.int32))
    density = (orbitals[:, None] * targets[None]).reshape((-1,) + targets.shape[1:])
    lines = transform(along_y, transform(along_z, density))
    lines = lax.all_to_all(lines, "slab", split_axis=2, concat_axis=1, tiled=True)
    lines = transform(along_x, kernel[None] * transform(along_x, lines))
    lines = lax.all_to_all(lines, "slab", split_axis=1, concat_axis=2, tiled=True)
    field = transform(along_z, transform(along_y, lines)).reshape((window,) + targets.shape)
    return -jnp.sum(field * orbitals[:, None], axis=0)


def solution(mesh):
    groups, slabs = mesh.shape["band"], mesh.shape["slab"]

    def shards(bands, occupied, occ_index, band_pick):
        picks, window = band_pick.shape[0], occ_index.shape[0]
        planes, points = bands.shape[1], bands.shape[2]
        fits = (
            window == 2
            and picks == 2
            and bands.shape[0] == picks
            and groups == 2 * CORES
            and slabs == CORES * picks * window
            and planes % 8 == 0
            and 2 * (points - LANES) == LANES
            and points == CORES * 2 * STEP * sum(SPLIT)
        )
        if fits:
            return by_layers(bands, occupied, occ_index, band_pick, groups, slabs)
        return by_lines(bands, occupied, occ_index, band_pick)

    placed = (P("band", "slab", None, None), P("band", "slab", None, None), P(), P("band"))
    return jax.shard_map(
        shards, mesh=mesh, in_specs=placed, out_specs=P("band", "slab", None, None), check_vma=False
    )
```

```python
import math

import jax
import jax.numpy as jnp
from jax import lax
from jax.experimental import pallas as pl
from jax.experimental.pallas import tpu as pltpu
from jax.sharding import PartitionSpec as P

grid_step = 0.25
omega = 0.106
CORES = 2
LANES = 128
STEP = 4
SPLIT = (4, 2, 2, 2, 2)
PARTS = ((0,), (1, 2), (3, 4))
BACK = 2
VMEM_LIMIT = 56 * 1024 * 1024


def wave_squared(modes, length):
    signed = jnp.where(modes <= length // 2, modes, modes - length)
    wave = 2.0 * math.pi / (length * grid_step) * signed.astype(jnp.float32)
    return wave * wave


def screened(squares):
    nonzero = jnp.where(squares > 0, squares, jnp.ones_like(squares))
    value = 4.0 * math.pi * (1.0 - jnp.exp(-squares / (4.0 * omega * omega))) / nonzero
    return jnp.where(squares > 0, value, jnp.full_like(squares, math.pi / (omega * omega)))


def cas_matrix(rows, columns, length):
    product = rows[:, None] * columns[None, :] % length
    phases = 2.0 * math.pi / length * product.astype(jnp.float32)
    return jnp.cos(phases) + jnp.sin(phases)


def halves(values):
    high = values.astype(jnp.bfloat16)
    low = (values - high.astype(jnp.float32)).astype(jnp.bfloat16)
    return high, low


def multiply(left, right):
    def dot(a, b):
        return jnp.dot(a, b, preferred_element_type=jnp.float32)

    return dot(left[0], right[0]) + (dot(left[0], right[1]) + dot(left[1], right[0]))


def multiply_deep(left, right):
    wide = jnp.concatenate([left[0], left[0], left[1]], axis=1)
    deep = jnp.concatenate([right[0], right[1], right[0]], axis=0)
    return jnp.dot(wide, deep, preferred_element_type=jnp.float32)


def pack_body(scalars, keep_ref, give_ref, keep_out, give_out):
    for source, out in ((keep_ref, keep_out), (give_ref, give_out)):
        rows = jnp.swapaxes(source[0], 0, 1)
        rows = rows.reshape((out.shape[1], 2, STEP) + rows.shape[1:])
        out[0, :, 0] = rows[:, 0, :, :, :LANES]
        out[0, :, 1] = rows[:, 1, :, :, :LANES]
        out[0, :, 2] = jnp.concatenate([rows[:, 0, :, :, LANES:], rows[:, 1, :, :, LANES:]], axis=-1)


def pack(stored, scalars, units, parts=1):
    count = scalars.shape[0] - 2
    planes, points = stored.shape[1], stored.shape[3]
    block = (1, units, 3, STEP, planes, LANES)
    rows = (1, planes, 2 * STEP * units, points)
    shape = jax.ShapeDtypeStruct((count, units * parts) + block[2:], jnp.float32)
    spec = pl.BlockSpec(block, lambda i, k, s: (i, k, 0, 0, 0, 0))
    return pl.pallas_call(
        pack_body,
        grid_spec=pltpu.PrefetchScalarGridSpec(
            num_scalar_prefetch=1,
            grid=(count, parts),
            in_specs=[
                pl.BlockSpec(rows, lambda i, k, s: (s[i], 0, s[count] + k, 0)),
                pl.BlockSpec(rows, lambda i, k, s: (s[i], 0, s[count + 1] + k, 0)),
            ],
            out_specs=[spec, spec],
        ),
        out_shape=[shape, shape],
        compiler_params=pltpu.CompilerParams(vmem_limit_bytes=VMEM_LIMIT),
        name="pack",
    )(scalars, stored, stored)


def unpack_body(scalars, keep_ref, got_ref, *rest):
    out = rest[-1]

    def place(source):
        tails = source[0, :, 2]
        lower = jnp.concatenate([source[0, :, 0], tails[..., : LANES // 2]], axis=-1)
        upper = jnp.concatenate([source[0, :, 1], tails[..., LANES // 2 :]], axis=-1)
        rows = jnp.stack([lower, upper], axis=1)
        out[0] = jnp.swapaxes(rows.reshape((-1,) + rows.shape[3:]), 0, 1)

    pl.when(pl.program_id(1) == 0)(lambda: place(keep_ref))
    pl.when(pl.program_id(1) == 1)(lambda: place(got_ref))


def unpack(keep, got, scalars, shape, earlier):
    count, units = keep.shape[:2]
    planes, points = shape[1], shape[3]
    spec = pl.BlockSpec((1,) + keep.shape[1:], lambda i, k, s: (i, 0, 0, 0, 0, 0))
    held = [] if earlier is None else [earlier]
    return pl.pallas_call(
        unpack_body,
        grid_spec=pltpu.PrefetchScalarGridSpec(
            num_scalar_prefetch=1,
            grid=(count, 2),
            in_specs=[spec, spec] + [pl.BlockSpec(memory_space=pl.ANY) for _ in held],
            out_specs=pl.BlockSpec(
                (1, planes, 2 * STEP * units, points), lambda i, k, s: (s[i], 0, s[count + k], 0)
            ),
        ),
        out_shape=jax.ShapeDtypeStruct(shape, jnp.float32),
        input_output_aliases={3: 0} if held else {},
        compiler_params=pltpu.CompilerParams(vmem_limit_bytes=VMEM_LIMIT),
        name="unpack",
    )(scalars, keep, got, *held)


def orbital_parts(same, first, second):
    pieces = range(first.shape[0])
    near = [jnp.where(same, first[d, 0], second[d, 0]) for d in pieces]
    far = [jnp.where(same, second[d, 0], first[d, 0]) for d in pieces]
    return near + far


def forward_body(scalars, near, far, first, second, lower_ref, upper_ref, planes_ref, keep_out, give_out):
    orbitals = orbital_parts(scalars[0] == 1, first, second)
    targets = [part[d, 0] for part in (near, far) for d in range(part.shape[0])]
    density = jnp.concatenate([t * o for t, o in zip(targets, orbitals)], axis=2)
    step, points = density.shape[1], density.shape[2]
    matrix = halves(planes_ref[...])
    results = []
    for part, weights in ((0, lower_ref), (1, upper_ref)):
        packed = jnp.concatenate([density[part], density[2]], axis=-1).reshape(step * points, 2 * LANES)
        lines = multiply_deep(halves(packed), halves(weights[...]))
        high, low = halves(lines)
        for row in range(step):
            where = slice(row * points, (row + 1) * points)
            results.append(multiply_deep(matrix, (high[where], low[where])))
    spectrum = jnp.swapaxes(jnp.stack(results), 0, 1)
    keep_out[...] = spectrum[: points // 2]
    give_out[...] = spectrum[points // 2 :]


def stacked(array, offset, layers):
    return pl.BlockSpec((layers, 1) + array.shape[2:], lambda u, s: (0, u + offset, 0, 0, 0, 0))


def forward(near, far, first, at, second, there, scalars, lower, upper, planes_matrix):
    units, points = near.shape[1], planes_matrix.shape[0]
    whole = lambda a: pl.BlockSpec(a.shape, lambda u, s: (0, 0))
    out = pl.BlockSpec((points // 2, 2 * STEP, points), lambda u, s: (0, u, 0))
    shape = jax.ShapeDtypeStruct((points // 2, 2 * STEP * units, points), jnp.float32)
    return pl.pallas_call(
        forward_body,
        grid_spec=pltpu.PrefetchScalarGridSpec(
            num_scalar_prefetch=1,
            grid=(units,),
            in_specs=[stacked(a, at, near.shape[0]) for a, at in ((near, 0), (far, 0), (first, at), (second, there))]
            + [whole(lower), whole(upper), whole(planes_matrix)],
            out_specs=[out, out],
        ),
        out_shape=[shape, shape],
        compiler_params=pltpu.CompilerParams(vmem_limit_bytes=VMEM_LIMIT),
        name="forward",
    )(scalars, near, far, first, second, lower, upper, planes_matrix)


def middle_body(count, kernel_ref, forth_ref, back_ref, *refs):
    ins, outs = refs[:count], refs[count:]
    forth, back = halves(forth_ref[...]), halves(back_ref[...])
    for k in range(kernel_ref.shape[0]):
        rows = jnp.concatenate([r[k] for r in ins], axis=0)
        spectrum = multiply(forth, halves(rows)) * kernel_ref[k]
        filtered = multiply(back, halves(spectrum))
        start = 0
        for out in outs:
            out[k] = filtered[start : start + out.shape[1]]
            start += out.shape[1]


def middle(spectra, kernel, forth, back):
    count = len(spectra)
    deep, _, points = spectra[0].shape
    block = 16
    parts = [pl.BlockSpec((block,) + a.shape[1:], lambda k: (k, 0, 0)) for a in spectra]
    whole = pl.BlockSpec((points, points), lambda k: (0, 0))
    return pl.pallas_call(
        lambda *refs: middle_body(count, *refs),
        grid=(deep // block,),
        in_specs=[pl.BlockSpec((block, points, points), lambda k: (k, 0, 0)), whole, whole] + parts,
        out_specs=parts,
        out_shape=[jax.ShapeDtypeStruct(a.shape, jnp.float32) for a in spectra],
        compiler_params=pltpu.CompilerParams(vmem_limit_bytes=VMEM_LIMIT),
        name="middle",
    )(kernel, forth, back, *spectra)


def inverse_body(scalars, keep_ref, got_ref, first, second, lower_ref, upper_ref, planes_ref, near, far):
    spectrum = jnp.swapaxes(jnp.concatenate([keep_ref[...], got_ref[...]], axis=0), 0, 1)
    points = spectrum.shape[1]
    step = spectrum.shape[0] // 2
    matrix = halves(planes_ref[...])
    packed = []
    for part, weights in ((0, lower_ref), (1, upper_ref)):
        lines = jnp.concatenate(
            [multiply(matrix, halves(spectrum[part * step + row])) for row in range(step)], axis=0
        )
        packed.append(multiply(halves(lines), halves(weights[...])).reshape(step, points, 2 * LANES))
    low, high = packed
    field = [low[:, :, :LANES], high[:, :, :LANES], low[:, :, LANES:] + high[:, :, LANES:]]
    orbitals = orbital_parts(scalars[0] == 1, first, second)
    outs = [(part, d) for part in (near, far) for d in range(part.shape[0])]
    planes = points // len(outs)
    for i, (orbital, (out, d)) in enumerate(zip(orbitals, outs)):
        for part in range(3):
            out[d, 0, part] = -field[part][:, i * planes : (i + 1) * planes] * orbital[part]


def inverse(keep, got, skip, units, first, at, second, there, scalars, lower, upper, planes_matrix):
    deep, _, points = keep.shape
    whole = lambda a: pl.BlockSpec(a.shape, lambda u, s: (0, 0))
    part = pl.BlockSpec((deep, 2 * STEP, points), lambda u, s: (0, u + skip, 0))
    layers = first.shape[0]
    shape = jax.ShapeDtypeStruct((layers, units) + first.shape[2:], jnp.float32)
    return pl.pallas_call(
        inverse_body,
        grid_spec=pltpu.PrefetchScalarGridSpec(
            num_scalar_prefetch=1,
            grid=(units,),
            in_specs=[part, part, stacked(first, at, layers), stacked(second, there, layers)]
            + [whole(lower), whole(upper), whole(planes_matrix)],
            out_specs=[stacked(shape, 0, layers)] * 2,
        ),
        out_shape=[shape] * 2,
        compiler_params=pltpu.CompilerParams(vmem_limit_bytes=VMEM_LIMIT),
        name="inverse",
    )(scalars, keep, got, first, second, lower, upper, planes_matrix)


def by_layers(bands, occupied, occ_index, band_pick, groups, slabs):
    picks, window = band_pick.shape[0], occ_index.shape[0]
    per_group, planes, points = occupied.shape[0], bands.shape[1], bands.shape[2]
    sides = window
    layers = slabs // sides
    half_rows = points // CORES
    units = half_rows // (2 * STEP)
    chunks = len(SPLIT)
    starts = [sum(SPLIT[:j]) for j in range(chunks)]

    band, slab = lax.axis_index("band"), lax.axis_index("slab")
    y, c = band // CORES, band % CORES
    z, x = slab // sides, slab % sides

    def swap(values, axis, size, flip):
        return lax.ppermute(values, axis, [(i, flip(i)) for i in range(size)])

    def over_core(values):
        return swap(values, "band", groups, lambda i: i ^ 1)

    def over_y(values):
        return swap(values, "band", groups, lambda i: i ^ CORES)

    def over_x(values):
        return swap(values, "slab", slabs, lambda i: i ^ 1)

    def over_z(values, d):
        return swap(values, "slab", slabs, lambda i: i ^ (d * sides))

    layer_of = z ^ jnp.arange(layers, dtype=jnp.int32)
    side_of = x ^ jnp.arange(sides, dtype=jnp.int32)
    slab_of = (side_of[:, None] + sides * layer_of[None, :]).reshape(-1)
    plane_of = (slab_of[:, None] * planes + jnp.arange(planes, dtype=jnp.int32)).reshape(-1)
    core_of = c ^ jnp.arange(CORES, dtype=jnp.int32)
    all_modes = jnp.arange(points, dtype=jnp.int32)
    mode_of = (core_of[:, None] * half_rows + jnp.arange(half_rows, dtype=jnp.int32)).reshape(-1)

    squares = wave_squared(all_modes, points)
    own_squares = wave_squared(c * half_rows + jnp.arange(half_rows, dtype=jnp.int32), points)

    first_bit = z % picks
    target_index = band_pick[jnp.arange(picks, dtype=jnp.int32) ^ first_bit]
    which = occ_index[side_of]
    owner = which // per_group
    owner_y, owner_core = owner // CORES, owner % CORES
    here = z // picks == c
    same = x == y
    flag = same.astype(jnp.int32)[None]

    def row_blocks(start, size):
        return jnp.stack([c * (units // size) + start // size, (1 - c) * (units // size) + start // size])

    def sync(*values):
        return lax.optimization_barrier(values)

    def after(value, *others):
        return lax.optimization_barrier((value,) + others)[0]

    def pack_orbital(h, parts, *earlier):
        start, size = starts[PARTS[h][0]], sum(SPLIT[j] for j in PARTS[h])
        scalars = jnp.concatenate([which % per_group, row_blocks(start, size)])
        return pack(occupied, after(scalars, *earlier), size, parts)

    def pack_target(j, parts, *earlier):
        scalars = jnp.concatenate([target_index, row_blocks(starts[j], SPLIT[j])])
        return pack(bands, after(scalars, *earlier), SPLIT[j], parts)


    def choose_orbital(keep, got):
        mine = jnp.where(owner_core[0] == c, keep[0], got[0])
        theirs = jnp.where(owner_core[1] == c, keep[1], got[1])
        return mine, theirs

    def choose_side(mine, other):
        return jnp.where(same, mine, other), jnp.where(same, other, mine)

    def choose_group(stay, got):
        return jnp.where(owner_y[0] == y, stay, got)

    def choose_targets(j, keep, got, carried=None):
        pieces = []
        begin = starts[j] - (starts[1] if j else 0)
        for d in range(layers):
            a, b = (keep, got) if d < picks else (got, keep)
            piece = jnp.where(here, a[d % picks], b[d % picks])[begin : begin + SPLIT[j]]
            if carried is not None and d and not d & (d - 1):
                piece = jnp.concatenate([piece, carried], axis=0)
            pieces.append(piece)
        return pieces

    def along_layers(pieces, carried=None):
        got, reached, size = [], [carried], pieces[0].shape[0]
        for d, piece in enumerate(pieces):
            moved = over_z(piece, d) if d else piece
            got.append(moved[:size])
            if carried is not None and d:
                reach = d & -d
                reached.append(over_z(reached[d - reach], reach) if d & (d - 1) else moved[size:])
        return got, reached

    size = SPLIT[0]
    keep, give = pack_target(0, 1)
    got = over_core(give)
    ready = choose_targets(0, keep, got)
    ready = sync(ready)[0]
    near0, _ = along_layers(ready)
    keep, give = pack_orbital(0, 1, ready)
    got = over_core(give)
    mine, theirs = choose_orbital(keep, got)
    other = over_x(theirs)
    stay, send = choose_side(mine, other)
    carried0 = choose_group(stay, over_y(send))
    keep, give = pack_orbital(1, 2, keep)
    mine, theirs = choose_orbital(keep, over_core(give))
    stay, send = choose_side(mine, over_x(theirs))
    keep, give = pack_target(1, chunks - 1, keep)
    got = over_core(give)
    ready = choose_targets(1, keep, got, carried0)
    ready, carried0, near0, stay, send, keep, got = sync(ready, carried0, near0, stay, send, keep, got)
    near1, first0 = along_layers(ready, carried0)
    near0 = jnp.stack(near0)
    far0 = over_x(near0)
    carried = choose_group(stay, over_y(send))
    carried1, carried2 = carried[:size], carried[size:]
    ready = choose_targets(2, keep, got, carried1)
    ready, carried1, carried2, near1, first0, far0 = sync(ready, carried1, carried2, near1, first0, far0)
    near2, first1 = along_layers(ready, carried1)
    first0, near1 = jnp.stack(first0), jnp.stack(near1)
    second0 = over_y(first0)
    far1 = over_x(near1)
    ready = choose_targets(3, keep, got, carried2)
    own_squares, squares, all_modes, mode_of, plane_of = after(
        (own_squares, squares, all_modes, mode_of, plane_of), near2[1]
    )
    kernel = screened(own_squares[:, None, None] + squares[None, :, None] + squares[None, None, :])
    kernel = kernel / float(points * points * points)
    columns = cas_matrix(all_modes, all_modes, points)
    empty = jnp.zeros((points - LANES, points), jnp.float32)
    lower = jnp.concatenate([columns, empty], axis=0)
    upper = jnp.concatenate([columns[:LANES], empty, columns[LANES:]], axis=0)
    lower_back = jnp.concatenate([columns, empty.T], axis=1)
    upper_back = jnp.concatenate([columns[:, :LANES], empty.T, columns[:, LANES:]], axis=1)
    to_modes = cas_matrix(mode_of, plane_of, points)
    to_planes = cas_matrix(plane_of, mode_of, points)
    forth = cas_matrix(all_modes, mode_of, points)
    back = cas_matrix(mode_of, all_modes, points)
    matrices = lower, upper, lower_back, upper_back, to_modes, to_planes, forth, back
    ready, carried2, near2, first1, far1, second0, kernel, matrices = sync(
        ready, carried2, near2, first1, far1, second0, kernel, matrices
    )
    lower, upper, lower_back, upper_back, to_modes, to_planes, forth, back = matrices
    near3, first2 = along_layers(ready, carried2)
    first1, near2 = jnp.stack(first1), jnp.stack(near2)
    second1 = over_y(first1)
    far2 = over_x(near2)
    ready = choose_targets(4, keep, got)
    keep0, give0 = forward(near0, far0, first0, 0, second0, 0, flag, lower, upper, to_modes)
    ready, near3, first2, second1, far2, keep0, give0 = sync(ready, near3, first2, second1, far2, keep0, give0)
    near4, _ = along_layers(ready)
    split = SPLIT[PARTS[2][0]]
    first3 = jnp.stack([piece[split:] for piece in first2])
    first2, near3 = jnp.stack([piece[:split] for piece in first2]), jnp.stack(near3)
    second2 = over_y(first2)
    far3 = over_x(near3)
    got0 = over_core(give0)
    keep1, give1 = forward(near1, far1, first1, 0, second1, 0, flag, lower, upper, to_modes)
    near4, far3, second2, first3, got0, keep1, give1 = sync(near4, far3, second2, first3, got0, keep1, give1)
    near4 = jnp.stack(near4)
    far4 = over_x(near4)
    second3 = over_y(first3)
    got1 = over_core(give1)
    keep2, give2 = forward(near2, far2, first1, SPLIT[1], second1, SPLIT[1], flag, lower, upper, to_modes)
    got2 = over_core(give2)
    keep3, give3 = forward(near3, far3, first2, 0, second2, 0, flag, lower, upper, to_modes)
    got3 = over_core(give3)
    keep4, give4 = forward(near4, far4, first3, 0, second3, 0, flag, lower, upper, to_modes)
    got4 = over_core(give4)

    spectra = [keep0, keep1, keep2, keep3, keep4, got0, got1, got2, got3, got4]
    filtered = middle(spectra, kernel, forth, back)

    orbit = [
        (first0, 0, second0, 0),
        (first1, 0, second1, 0),
        (first1, SPLIT[1], second1, SPLIT[1]),
        (first2, 0, second2, 0),
        (first3, 0, second3, 0),
    ]
    back_got = [over_core(values) for values in filtered[chunks:]]
    queue = [(j, skip) for j in range(chunks) for skip in range(0, SPLIT[j], BACK)]
    queue.reverse()
    result, home, sums = None, None, None
    for turn in range(len(queue) + 2):
        near = far = got = pieces = None
        if turn < len(queue):
            j, skip = queue[turn]
            first, at, second, there = orbit[j]
            orbitals = first, at + skip, second, there + skip
            near, far = inverse(
                filtered[j], back_got[j], skip, BACK, *orbitals, flag, lower_back, upper_back, to_planes
            )
        if turn:
            near, far, sums, home, result = sync(near, far, sums, home, result)
        if far is not None:
            got = over_x(far)
        if sums is not None:
            pieces = [sums[0][d] + sums[1][d] for d in range(layers)]
            pieces = [over_z(piece, d) if d else piece for d, piece in enumerate(pieces)]
        if home is not None:
            j, skip = queue[turn - 2]
            kept, sent = jnp.stack(home[:picks]), jnp.stack(home[picks:])
            own = jnp.where(here, kept, sent)
            other = over_core(jnp.where(here, sent, kept))
            index = jnp.arange(picks, dtype=jnp.int32) ^ first_bit
            place = jnp.concatenate([index, row_blocks(starts[j] + skip, BACK)])
            result = unpack(own, other, place, (picks,) + bands.shape[1:], result)
        sums = None if far is None else (near, got)
        home = pieces
    return result


def broadcast(x, axis, root):
    mine = lax.axis_index(axis) == root
    return lax.psum(jnp.where(mine, x, jnp.zeros_like(x)), axis)


def by_lines(bands, occupied, occ_index, band_pick):
    points, planes = bands.shape[2], bands.shape[1]
    window, per_group = occ_index.shape[0], occupied.shape[0]
    modes = jnp.arange(points, dtype=jnp.int32)
    matrix = cas_matrix(modes, modes, points)
    squares = wave_squared(modes, points)

    def transform(pattern, values):
        return jnp.einsum(pattern, values, matrix, precision=lax.Precision.HIGHEST)

    along_z, along_y, along_x = "pxyz,zk->pxyk", "pxyz,yk->pxkz", "pxyz,xk->pkyz"
    offset = lax.axis_index("slab") * planes
    row_squares = lax.dynamic_slice_in_dim(squares, offset, planes)
    kernel = screened(squares[:, None, None] + row_squares[None, :, None] + squares[None, None, :])
    kernel = kernel / float(points * points * points)
    targets = jnp.take(bands, band_pick, axis=0)

    def fetch_orbital(turn):
        which = occ_index[turn]
        own_orbital = lax.dynamic_index_in_dim(occupied, which % per_group, 0, keepdims=False)
        return broadcast(own_orbital, "band", which // per_group)

    orbitals = lax.map(fetch_orbital, jnp.arange(window, dtype=jnp.int32))
    density = (orbitals[:, None] * targets[None]).reshape((-1,) + targets.shape[1:])
    lines = transform(along_y, transform(along_z, density))
    lines = lax.all_to_all(lines, "slab", split_axis=2, concat_axis=1, tiled=True)
    lines = transform(along_x, kernel[None] * transform(along_x, lines))
    lines = lax.all_to_all(lines, "slab", split_axis=1, concat_axis=2, tiled=True)
    field = transform(along_z, transform(along_y, lines)).reshape((window,) + targets.shape)
    return -jnp.sum(field * orbitals[:, None], axis=0)


def solution(mesh):
    groups, slabs = mesh.shape["band"], mesh.shape["slab"]

    def shards(bands, occupied, occ_index, band_pick):
        picks, window = band_pick.shape[0], occ_index.shape[0]
        planes, points = bands.shape[1], bands.shape[2]
        fits = (
            window == 2
            and picks == 2
            and bands.shape[0] == picks
            and groups == 2 * CORES
            and slabs == CORES * picks * window
            and planes % 8 == 0
            and 2 * (points - LANES) == LANES
            and points == CORES * 2 * STEP * sum(SPLIT)
        )
        if fits:
            return by_layers(bands, occupied, occ_index, band_pick, groups, slabs)
        return by_lines(bands, occupied, occ_index, band_pick)

    placed = (P("band", "slab", None, None), P("band", "slab", None, None), P(), P("band"))
    return jax.shard_map(
        shards, mesh=mesh, in_specs=placed, out_specs=P("band", "slab", None, None), check_vma=False
    )
```

```python
import math

import jax
import jax.numpy as jnp
from jax import lax
from jax.experimental import pallas as pl
from jax.experimental.pallas import tpu as pltpu
from jax.sharding import PartitionSpec as P

grid_step = 0.25
omega = 0.106
CORES = 2
LANES = 128
STEP = 4
SPLIT = (4, 2, 2, 2, 2)
PARTS = ((0,), (1, 2), (3, 4))
BACK = 2
VMEM_LIMIT = 16 * 1024 * 1024
PACK_LIMIT = 56 * 1024 * 1024


def wave_squared(modes, length):
    signed = jnp.where(modes <= length // 2, modes, modes - length)
    wave = 2.0 * math.pi / (length * grid_step) * signed.astype(jnp.float32)
    return wave * wave


def screened(squares):
    nonzero = jnp.where(squares > 0, squares, jnp.ones_like(squares))
    value = 4.0 * math.pi * (1.0 - jnp.exp(-squares / (4.0 * omega * omega))) / nonzero
    return jnp.where(squares > 0, value, jnp.full_like(squares, math.pi / (omega * omega)))


def cas_matrix(rows, columns, length):
    product = rows[:, None] * columns[None, :] % length
    phases = 2.0 * math.pi / length * product.astype(jnp.float32)
    return jnp.cos(phases) + jnp.sin(phases)


def halves(values):
    high = values.astype(jnp.bfloat16)
    low = (values - high.astype(jnp.float32)).astype(jnp.bfloat16)
    return high, low


def multiply(left, right):
    def dot(a, b):
        return jnp.dot(a, b, preferred_element_type=jnp.float32)

    return dot(left[0], right[0]) + (dot(left[0], right[1]) + dot(left[1], right[0]))


def multiply_deep(left, right):
    wide = jnp.concatenate([left[0], left[0], left[1]], axis=1)
    deep = jnp.concatenate([right[0], right[1], right[0]], axis=0)
    return jnp.dot(wide, deep, preferred_element_type=jnp.float32)


def pack_body(scalars, keep_ref, give_ref, keep_out, give_out):
    for source, out in ((keep_ref, keep_out), (give_ref, give_out)):
        rows = jnp.swapaxes(source[0], 0, 1)
        rows = rows.reshape((out.shape[1], 2, STEP) + rows.shape[1:])
        out[0, :, 0] = rows[:, 0, :, :, :LANES]
        out[0, :, 1] = rows[:, 1, :, :, :LANES]
        out[0, :, 2] = jnp.concatenate([rows[:, 0, :, :, LANES:], rows[:, 1, :, :, LANES:]], axis=-1)


def pack(stored, scalars, units, parts=1):
    count = scalars.shape[0] - 2
    planes, points = stored.shape[1], stored.shape[3]
    block = (1, units, 3, STEP, planes, LANES)
    rows = (1, planes, 2 * STEP * units, points)
    shape = jax.ShapeDtypeStruct((count, units * parts) + block[2:], jnp.float32)
    spec = pl.BlockSpec(block, lambda i, k, s: (i, k, 0, 0, 0, 0))
    return pl.pallas_call(
        pack_body,
        grid_spec=pltpu.PrefetchScalarGridSpec(
            num_scalar_prefetch=1,
            grid=(count, parts),
            in_specs=[
                pl.BlockSpec(rows, lambda i, k, s: (s[i], 0, s[count] + k, 0)),
                pl.BlockSpec(rows, lambda i, k, s: (s[i], 0, s[count + 1] + k, 0)),
            ],
            out_specs=[spec, spec],
        ),
        out_shape=[shape, shape],
        compiler_params=pltpu.CompilerParams(vmem_limit_bytes=PACK_LIMIT),
        name="pack",
    )(scalars, stored, stored)


def unpack_body(scalars, keep_ref, got_ref, *rest):
    out = rest[-1]

    def place(source):
        tails = source[0, :, 2]
        lower = jnp.concatenate([source[0, :, 0], tails[..., : LANES // 2]], axis=-1)
        upper = jnp.concatenate([source[0, :, 1], tails[..., LANES // 2 :]], axis=-1)
        rows = jnp.stack([lower, upper], axis=1)
        out[0] = jnp.swapaxes(rows.reshape((-1,) + rows.shape[3:]), 0, 1)

    pl.when(pl.program_id(1) == 0)(lambda: place(keep_ref))
    pl.when(pl.program_id(1) == 1)(lambda: place(got_ref))


def unpack(keep, got, scalars, shape, earlier):
    count, units = keep.shape[:2]
    planes, points = shape[1], shape[3]
    spec = pl.BlockSpec((1,) + keep.shape[1:], lambda i, k, s: (i, 0, 0, 0, 0, 0))
    held = [] if earlier is None else [earlier]
    return pl.pallas_call(
        unpack_body,
        grid_spec=pltpu.PrefetchScalarGridSpec(
            num_scalar_prefetch=1,
            grid=(count, 2),
            in_specs=[spec, spec] + [pl.BlockSpec(memory_space=pl.ANY) for _ in held],
            out_specs=pl.BlockSpec(
                (1, planes, 2 * STEP * units, points), lambda i, k, s: (s[i], 0, s[count + k], 0)
            ),
        ),
        out_shape=jax.ShapeDtypeStruct(shape, jnp.float32),
        input_output_aliases={3: 0} if held else {},
        compiler_params=pltpu.CompilerParams(vmem_limit_bytes=VMEM_LIMIT),
        name="unpack",
    )(scalars, keep, got, *held)


def orbital_parts(same, first, second):
    pieces = range(first.shape[0])
    near = [jnp.where(same, first[d, 0], second[d, 0]) for d in pieces]
    far = [jnp.where(same, second[d, 0], first[d, 0]) for d in pieces]
    return near + far


def forward_body(scalars, near, far, first, second, lower_ref, upper_ref, planes_ref, keep_out, give_out):
    orbitals = orbital_parts(scalars[0] == 1, first, second)
    targets = [part[d, 0] for part in (near, far) for d in range(part.shape[0])]
    density = jnp.concatenate([t * o for t, o in zip(targets, orbitals)], axis=2)
    step, points = density.shape[1], density.shape[2]
    matrix = halves(planes_ref[...])
    results = []
    for part, weights in ((0, lower_ref), (1, upper_ref)):
        packed = jnp.concatenate([density[part], density[2]], axis=-1).reshape(step * points, 2 * LANES)
        lines = multiply_deep(halves(packed), halves(weights[...]))
        high, low = halves(lines)
        for row in range(step):
            where = slice(row * points, (row + 1) * points)
            results.append(multiply_deep(matrix, (high[where], low[where])))
    spectrum = jnp.swapaxes(jnp.stack(results), 0, 1)
    keep_out[...] = spectrum[: points // 2]
    give_out[...] = spectrum[points // 2 :]


def stacked(array, offset, layers):
    return pl.BlockSpec((layers, 1) + array.shape[2:], lambda u, s: (0, u + offset, 0, 0, 0, 0))


def forward(near, far, first, at, second, there, scalars, lower, upper, planes_matrix):
    units, points = near.shape[1], planes_matrix.shape[0]
    whole = lambda a: pl.BlockSpec(a.shape, lambda u, s: (0, 0))
    out = pl.BlockSpec((points // 2, 2 * STEP, points), lambda u, s: (0, u, 0))
    shape = jax.ShapeDtypeStruct((points // 2, 2 * STEP * units, points), jnp.float32)
    return pl.pallas_call(
        forward_body,
        grid_spec=pltpu.PrefetchScalarGridSpec(
            num_scalar_prefetch=1,
            grid=(units,),
            in_specs=[stacked(a, at, near.shape[0]) for a, at in ((near, 0), (far, 0), (first, at), (second, there))]
            + [whole(lower), whole(upper), whole(planes_matrix)],
            out_specs=[out, out],
        ),
        out_shape=[shape, shape],
        compiler_params=pltpu.CompilerParams(vmem_limit_bytes=VMEM_LIMIT),
        name="forward",
    )(scalars, near, far, first, second, lower, upper, planes_matrix)


def middle_body(count, kernel_ref, forth_ref, back_ref, *refs):
    ins, outs = refs[:count], refs[count:]
    forth, back = halves(forth_ref[...]), halves(back_ref[...])
    for k in range(kernel_ref.shape[0]):
        rows = jnp.concatenate([r[k] for r in ins], axis=0)
        spectrum = multiply(forth, halves(rows)) * kernel_ref[k]
        filtered = multiply(back, halves(spectrum))
        start = 0
        for out in outs:
            out[k] = filtered[start : start + out.shape[1]]
            start += out.shape[1]


def middle(spectra, kernel, forth, back):
    count = len(spectra)
    deep, _, points = spectra[0].shape
    block = 16
    parts = [pl.BlockSpec((block,) + a.shape[1:], lambda k: (k, 0, 0)) for a in spectra]
    whole = pl.BlockSpec((points, points), lambda k: (0, 0))
    return pl.pallas_call(
        lambda *refs: middle_body(count, *refs),
        grid=(deep // block,),
        in_specs=[pl.BlockSpec((block, points, points), lambda k: (k, 0, 0)), whole, whole] + parts,
        out_specs=parts,
        out_shape=[jax.ShapeDtypeStruct(a.shape, jnp.float32) for a in spectra],
        compiler_params=pltpu.CompilerParams(vmem_limit_bytes=VMEM_LIMIT),
        name="middle",
    )(kernel, forth, back, *spectra)


def inverse_body(scalars, keep_ref, got_ref, first, second, lower_ref, upper_ref, planes_ref, near, far):
    spectrum = jnp.swapaxes(jnp.concatenate([keep_ref[...], got_ref[...]], axis=0), 0, 1)
    points = spectrum.shape[1]
    step = spectrum.shape[0] // 2
    matrix = halves(planes_ref[...])
    packed = []
    for part, weights in ((0, lower_ref), (1, upper_ref)):
        lines = jnp.concatenate(
            [multiply(matrix, halves(spectrum[part * step + row])) for row in range(step)], axis=0
        )
        packed.append(multiply(halves(lines), halves(weights[...])).reshape(step, points, 2 * LANES))
    low, high = packed
    field = [low[:, :, :LANES], high[:, :, :LANES], low[:, :, LANES:] + high[:, :, LANES:]]
    orbitals = orbital_parts(scalars[0] == 1, first, second)
    outs = [(part, d) for part in (near, far) for d in range(part.shape[0])]
    planes = points // len(outs)
    for i, (orbital, (out, d)) in enumerate(zip(orbitals, outs)):
        for part in range(3):
            out[d, 0, part] = -field[part][:, i * planes : (i + 1) * planes] * orbital[part]


def inverse(keep, got, skip, units, first, at, second, there, scalars, lower, upper, planes_matrix):
    deep, _, points = keep.shape
    whole = lambda a: pl.BlockSpec(a.shape, lambda u, s: (0, 0))
    part = pl.BlockSpec((deep, 2 * STEP, points), lambda u, s: (0, u + skip, 0))
    layers = first.shape[0]
    shape = jax.ShapeDtypeStruct((layers, units) + first.shape[2:], jnp.float32)
    return pl.pallas_call(
        inverse_body,
        grid_spec=pltpu.PrefetchScalarGridSpec(
            num_scalar_prefetch=1,
            grid=(units,),
            in_specs=[part, part, stacked(first, at, layers), stacked(second, there, layers)]
            + [whole(lower), whole(upper), whole(planes_matrix)],
            out_specs=[stacked(shape, 0, layers)] * 2,
        ),
        out_shape=[shape] * 2,
        compiler_params=pltpu.CompilerParams(vmem_limit_bytes=VMEM_LIMIT),
        name="inverse",
    )(scalars, keep, got, first, second, lower, upper, planes_matrix)


def by_layers(bands, occupied, occ_index, band_pick, groups, slabs):
    picks, window = band_pick.shape[0], occ_index.shape[0]
    per_group, planes, points = occupied.shape[0], bands.shape[1], bands.shape[2]
    sides = window
    layers = slabs // sides
    half_rows = points // CORES
    units = half_rows // (2 * STEP)
    chunks = len(SPLIT)
    starts = [sum(SPLIT[:j]) for j in range(chunks)]

    band, slab = lax.axis_index("band"), lax.axis_index("slab")
    y, c = band // CORES, band % CORES
    z, x = slab // sides, slab % sides

    def swap(values, axis, size, flip):
        return lax.ppermute(values, axis, [(i, flip(i)) for i in range(size)])

    def over_core(values):
        return swap(values, "band", groups, lambda i: i ^ 1)

    def over_y(values):
        return swap(values, "band", groups, lambda i: i ^ CORES)

    def over_x(values):
        return swap(values, "slab", slabs, lambda i: i ^ 1)

    def over_z(values, d):
        return swap(values, "slab", slabs, lambda i: i ^ (d * sides))

    layer_of = z ^ jnp.arange(layers, dtype=jnp.int32)
    side_of = x ^ jnp.arange(sides, dtype=jnp.int32)
    slab_of = (side_of[:, None] + sides * layer_of[None, :]).reshape(-1)
    plane_of = (slab_of[:, None] * planes + jnp.arange(planes, dtype=jnp.int32)).reshape(-1)
    core_of = c ^ jnp.arange(CORES, dtype=jnp.int32)
    all_modes = jnp.arange(points, dtype=jnp.int32)
    mode_of = (core_of[:, None] * half_rows + jnp.arange(half_rows, dtype=jnp.int32)).reshape(-1)

    squares = wave_squared(all_modes, points)
    own_squares = wave_squared(c * half_rows + jnp.arange(half_rows, dtype=jnp.int32), points)

    first_bit = z % picks
    target_index = band_pick[jnp.arange(picks, dtype=jnp.int32) ^ first_bit]
    which = occ_index[side_of]
    owner = which // per_group
    owner_y, owner_core = owner // CORES, owner % CORES
    here = z // picks == c
    same = x == y
    flag = same.astype(jnp.int32)[None]

    def row_blocks(start, size):
        return jnp.stack([c * (units // size) + start // size, (1 - c) * (units // size) + start // size])

    def sync(*values):
        return lax.optimization_barrier(values)

    def after(value, *others):
        return lax.optimization_barrier((value,) + others)[0]

    def pack_orbital(h, parts, *earlier):
        start, size = starts[PARTS[h][0]], sum(SPLIT[j] for j in PARTS[h])
        scalars = jnp.concatenate([which % per_group, row_blocks(start, size)])
        return pack(occupied, after(scalars, *earlier), size, parts)

    def pack_target(j, parts, *earlier):
        scalars = jnp.concatenate([target_index, row_blocks(starts[j], SPLIT[j])])
        return pack(bands, after(scalars, *earlier), SPLIT[j], parts)


    def choose_orbital(keep, got):
        mine = jnp.where(owner_core[0] == c, keep[0], got[0])
        theirs = jnp.where(owner_core[1] == c, keep[1], got[1])
        return mine, theirs

    def choose_side(mine, other):
        return jnp.where(same, mine, other), jnp.where(same, other, mine)

    def choose_group(stay, got):
        return jnp.where(owner_y[0] == y, stay, got)

    def choose_targets(j, keep, got, carried=None):
        pieces = []
        begin = starts[j] - (starts[1] if j else 0)
        for d in range(layers):
            a, b = (keep, got) if d < picks else (got, keep)
            piece = jnp.where(here, a[d % picks], b[d % picks])[begin : begin + SPLIT[j]]
            if carried is not None and d and not d & (d - 1):
                piece = jnp.concatenate([piece, carried], axis=0)
            pieces.append(piece)
        return pieces

    def along_layers(pieces, carried=None):
        got, reached, size = [], [carried], pieces[0].shape[0]
        for d, piece in enumerate(pieces):
            moved = over_z(piece, d) if d else piece
            got.append(moved[:size])
            if carried is not None and d:
                reach = d & -d
                reached.append(over_z(reached[d - reach], reach) if d & (d - 1) else moved[size:])
        return got, reached

    size = SPLIT[0]
    keep, give = pack_target(0, 1)
    got = over_core(give)
    ready = choose_targets(0, keep, got)
    ready = sync(ready)[0]
    near0, _ = along_layers(ready)
    keep, give = pack_orbital(0, 1, ready)
    got = over_core(give)
    mine, theirs = choose_orbital(keep, got)
    other = over_x(theirs)
    stay, send = choose_side(mine, other)
    carried0 = choose_group(stay, over_y(send))
    keep, give = pack_orbital(1, 2, keep)
    mine, theirs = choose_orbital(keep, over_core(give))
    stay, send = choose_side(mine, over_x(theirs))
    keep, give = pack_target(1, chunks - 1, keep)
    got = over_core(give)
    ready = choose_targets(1, keep, got, carried0)
    ready, carried0, near0, stay, send, keep, got = sync(ready, carried0, near0, stay, send, keep, got)
    near1, first0 = along_layers(ready, carried0)
    near0 = jnp.stack(near0)
    far0 = over_x(near0)
    carried = choose_group(stay, over_y(send))
    carried1, carried2 = carried[:size], carried[size:]
    ready = choose_targets(2, keep, got, carried1)
    ready, carried1, carried2, near1, first0, far0 = sync(ready, carried1, carried2, near1, first0, far0)
    near2, first1 = along_layers(ready, carried1)
    first0, near1 = jnp.stack(first0), jnp.stack(near1)
    second0 = over_y(first0)
    far1 = over_x(near1)
    ready = choose_targets(3, keep, got, carried2)
    own_squares, squares, all_modes, mode_of, plane_of = after(
        (own_squares, squares, all_modes, mode_of, plane_of), near2[1]
    )
    kernel = screened(own_squares[:, None, None] + squares[None, :, None] + squares[None, None, :])
    kernel = kernel / float(points * points * points)
    columns = cas_matrix(all_modes, all_modes, points)
    empty = jnp.zeros((points - LANES, points), jnp.float32)
    lower = jnp.concatenate([columns, empty], axis=0)
    upper = jnp.concatenate([columns[:LANES], empty, columns[LANES:]], axis=0)
    lower_back = jnp.concatenate([columns, empty.T], axis=1)
    upper_back = jnp.concatenate([columns[:, :LANES], empty.T, columns[:, LANES:]], axis=1)
    to_modes = cas_matrix(mode_of, plane_of, points)
    to_planes = cas_matrix(plane_of, mode_of, points)
    forth = cas_matrix(all_modes, mode_of, points)
    back = cas_matrix(mode_of, all_modes, points)
    matrices = lower, upper, lower_back, upper_back, to_modes, to_planes, forth, back
    ready, carried2, near2, first1, far1, second0, kernel, matrices = sync(
        ready, carried2, near2, first1, far1, second0, kernel, matrices
    )
    lower, upper, lower_back, upper_back, to_modes, to_planes, forth, back = matrices
    near3, first2 = along_layers(ready, carried2)
    first1, near2 = jnp.stack(first1), jnp.stack(near2)
    second1 = over_y(first1)
    far2 = over_x(near2)
    ready = choose_targets(4, keep, got)
    keep0, give0 = forward(near0, far0, first0, 0, second0, 0, flag, lower, upper, to_modes)
    ready, near3, first2, second1, far2, keep0, give0 = sync(ready, near3, first2, second1, far2, keep0, give0)
    near4, _ = along_layers(ready)
    split = SPLIT[PARTS[2][0]]
    first3 = jnp.stack([piece[split:] for piece in first2])
    first2, near3 = jnp.stack([piece[:split] for piece in first2]), jnp.stack(near3)
    second2 = over_y(first2)
    far3 = over_x(near3)
    got0 = over_core(give0)
    keep1, give1 = forward(near1, far1, first1, 0, second1, 0, flag, lower, upper, to_modes)
    near4, far3, second2, first3, got0, keep1, give1 = sync(near4, far3, second2, first3, got0, keep1, give1)
    cut = SPLIT[4] // 2
    near4 = [jnp.stack([piece[at : at + cut] for piece in near4]) for at in (0, cut)]
    far4 = [over_x(near4[0])]
    far4.append(over_x(near4[1]))
    second3 = over_y(first3)
    got1 = over_core(give1)
    keep2, give2 = forward(near2, far2, first1, SPLIT[1], second1, SPLIT[1], flag, lower, upper, to_modes)
    got2 = over_core(give2)
    keep3, give3 = forward(near3, far3, first2, 0, second2, 0, flag, lower, upper, to_modes)
    got3 = over_core(give3)
    keep4, give4 = forward(near4[0], far4[0], first3, 0, second3, 0, flag, lower, upper, to_modes)
    got4 = over_core(give4)
    keep5, give5 = forward(near4[1], far4[1], first3, cut, second3, cut, flag, lower, upper, to_modes)
    got5 = over_core(give5)

    spectra = [keep0, keep1, keep2, keep3, keep4, keep5, got0, got1, got2, got3, got4, got5]
    filtered = middle(spectra, kernel, forth, back)

    orbit = [
        (first0, 0, second0, 0),
        (first1, 0, second1, 0),
        (first1, SPLIT[1], second1, SPLIT[1]),
        (first2, 0, second2, 0),
        (first3, 0, second3, 0),
    ]
    back_got = [over_core(values) for values in filtered[chunks + 1 :]]
    queue = [(j, skip, BACK) for j in range(chunks - 1) for skip in range(0, SPLIT[j], BACK)]
    queue = [(chunks, 0, cut), (chunks - 1, 0, cut)] + queue[::-1]
    orbit.append((first3, cut, second3, cut))
    starts.append(starts[-1] + cut)
    result, home, sums = None, None, None
    for turn in range(len(queue) + 2):
        near = far = got = pieces = None
        if turn < len(queue):
            j, skip, count = queue[turn]
            first, at, second, there = orbit[j]
            orbitals = first, at + skip, second, there + skip
            near, far = inverse(
                filtered[j], back_got[j], skip, count, *orbitals, flag, lower_back, upper_back, to_planes
            )
        if turn:
            near, far, sums, home, result = sync(near, far, sums, home, result)
        if far is not None:
            got = over_x(far)
        if sums is not None:
            pieces = [sums[0][d] + sums[1][d] for d in range(layers)]
            pieces = [over_z(piece, d) if d else piece for d, piece in enumerate(pieces)]
        if home is not None:
            j, skip, count = queue[turn - 2]
            kept, sent = jnp.stack(home[:picks]), jnp.stack(home[picks:])
            own = jnp.where(here, kept, sent)
            other = over_core(jnp.where(here, sent, kept))
            index = jnp.arange(picks, dtype=jnp.int32) ^ first_bit
            place = jnp.concatenate([index, row_blocks(starts[j] + skip, count)])
            result = unpack(own, other, place, (picks,) + bands.shape[1:], result)
        sums = None if far is None else (near, got)
        home = pieces
    return result


def broadcast(x, axis, root):
    mine = lax.axis_index(axis) == root
    return lax.psum(jnp.where(mine, x, jnp.zeros_like(x)), axis)


def by_lines(bands, occupied, occ_index, band_pick):
    points, planes = bands.shape[2], bands.shape[1]
    window, per_group = occ_index.shape[0], occupied.shape[0]
    modes = jnp.arange(points, dtype=jnp.int32)
    matrix = cas_matrix(modes, modes, points)
    squares = wave_squared(modes, points)

    def transform(pattern, values):
        return jnp.einsum(pattern, values, matrix, precision=lax.Precision.HIGHEST)

    along_z, along_y, along_x = "pxyz,zk->pxyk", "pxyz,yk->pxkz", "pxyz,xk->pkyz"
    offset = lax.axis_index("slab") * planes
    row_squares = lax.dynamic_slice_in_dim(squares, offset, planes)
    kernel = screened(squares[:, None, None] + row_squares[None, :, None] + squares[None, None, :])
    kernel = kernel / float(points * points * points)
    targets = jnp.take(bands, band_pick, axis=0)

    def fetch_orbital(turn):
        which = occ_index[turn]
        own_orbital = lax.dynamic_index_in_dim(occupied, which % per_group, 0, keepdims=False)
        return broadcast(own_orbital, "band", which // per_group)

    orbitals = lax.map(fetch_orbital, jnp.arange(window, dtype=jnp.int32))
    density = (orbitals[:, None] * targets[None]).reshape((-1,) + targets.shape[1:])
    lines = transform(along_y, transform(along_z, density))
    lines = lax.all_to_all(lines, "slab", split_axis=2, concat_axis=1, tiled=True)
    lines = transform(along_x, kernel[None] * transform(along_x, lines))
    lines = lax.all_to_all(lines, "slab", split_axis=1, concat_axis=2, tiled=True)
    field = transform(along_z, transform(along_y, lines)).reshape((window,) + targets.shape)
    return -jnp.sum(field * orbitals[:, None], axis=0)


def solution(mesh):
    groups, slabs = mesh.shape["band"], mesh.shape["slab"]

    def shards(bands, occupied, occ_index, band_pick):
        picks, window = band_pick.shape[0], occ_index.shape[0]
        planes, points = bands.shape[1], bands.shape[2]
        fits = (
            window == 2
            and picks == 2
            and bands.shape[0] == picks
            and groups == 2 * CORES
            and slabs == CORES * picks * window
            and planes % 8 == 0
            and 2 * (points - LANES) == LANES
            and points == CORES * 2 * STEP * sum(SPLIT)
        )
        if fits:
            return by_layers(bands, occupied, occ_index, band_pick, groups, slabs)
        return by_lines(bands, occupied, occ_index, band_pick)

    placed = (P("band", "slab", None, None), P("band", "slab", None, None), P(), P("band"))
    return jax.shard_map(
        shards, mesh=mesh, in_specs=placed, out_specs=P("band", "slab", None, None), check_vma=False
    )
```

```python
import math

import jax
import jax.numpy as jnp
from jax import lax
from jax.experimental import pallas as pl
from jax.experimental.pallas import tpu as pltpu
from jax.sharding import PartitionSpec as P

grid_step = 0.25
omega = 0.106
CORES = 2
LANES = 128
STEP = 4
SPLIT = (4, 2, 2, 2, 2)
PARTS = ((0,), (1, 2), (3, 4))
BACK = 2
VMEM_LIMIT = 16 * 1024 * 1024
PACK_LIMIT = 56 * 1024 * 1024


def wave_squared(modes, length):
    signed = jnp.where(modes <= length // 2, modes, modes - length)
    wave = 2.0 * math.pi / (length * grid_step) * signed.astype(jnp.float32)
    return wave * wave


def screened(squares):
    nonzero = jnp.where(squares > 0, squares, jnp.ones_like(squares))
    value = 4.0 * math.pi * (1.0 - jnp.exp(-squares / (4.0 * omega * omega))) / nonzero
    return jnp.where(squares > 0, value, jnp.full_like(squares, math.pi / (omega * omega)))


def cas_matrix(rows, columns, length):
    product = rows[:, None] * columns[None, :] % length
    phases = 2.0 * math.pi / length * product.astype(jnp.float32)
    return jnp.cos(phases) + jnp.sin(phases)


def halves(values):
    high = values.astype(jnp.bfloat16)
    low = (values - high.astype(jnp.float32)).astype(jnp.bfloat16)
    return high, low


def multiply(left, right):
    def dot(a, b):
        return jnp.dot(a, b, preferred_element_type=jnp.float32)

    return dot(left[0], right[0]) + (dot(left[0], right[1]) + dot(left[1], right[0]))


def multiply_deep(left, right):
    wide = jnp.concatenate([left[0], left[0], left[1]], axis=1)
    deep = jnp.concatenate([right[0], right[1], right[0]], axis=0)
    return jnp.dot(wide, deep, preferred_element_type=jnp.float32)


def pack_body(scalars, keep_ref, give_ref, keep_out, give_out):
    for source, out in ((keep_ref, keep_out), (give_ref, give_out)):
        rows = jnp.swapaxes(source[0], 0, 1)
        rows = rows.reshape((out.shape[1], 2, STEP) + rows.shape[1:])
        out[0, :, 0] = rows[:, 0, :, :, :LANES]
        out[0, :, 1] = rows[:, 1, :, :, :LANES]
        out[0, :, 2] = jnp.concatenate([rows[:, 0, :, :, LANES:], rows[:, 1, :, :, LANES:]], axis=-1)


def pack(stored, scalars, units, parts=1):
    count = scalars.shape[0] - 2
    planes, points = stored.shape[1], stored.shape[3]
    block = (1, units, 3, STEP, planes, LANES)
    rows = (1, planes, 2 * STEP * units, points)
    shape = jax.ShapeDtypeStruct((count, units * parts) + block[2:], jnp.float32)
    spec = pl.BlockSpec(block, lambda i, k, s: (i, k, 0, 0, 0, 0))
    return pl.pallas_call(
        pack_body,
        grid_spec=pltpu.PrefetchScalarGridSpec(
            num_scalar_prefetch=1,
            grid=(count, parts),
            in_specs=[
                pl.BlockSpec(rows, lambda i, k, s: (s[i], 0, s[count] + k, 0)),
                pl.BlockSpec(rows, lambda i, k, s: (s[i], 0, s[count + 1] + k, 0)),
            ],
            out_specs=[spec, spec],
        ),
        out_shape=[shape, shape],
        compiler_params=pltpu.CompilerParams(vmem_limit_bytes=PACK_LIMIT),
        name="pack",
    )(scalars, stored, stored)


def unpack_body(scalars, keep_ref, got_ref, *rest):
    out = rest[-1]

    def place(source):
        tails = source[0, :, 2]
        lower = jnp.concatenate([source[0, :, 0], tails[..., : LANES // 2]], axis=-1)
        upper = jnp.concatenate([source[0, :, 1], tails[..., LANES // 2 :]], axis=-1)
        rows = jnp.stack([lower, upper], axis=1)
        out[0] = jnp.swapaxes(rows.reshape((-1,) + rows.shape[3:]), 0, 1)

    pl.when(pl.program_id(1) == 0)(lambda: place(keep_ref))
    pl.when(pl.program_id(1) == 1)(lambda: place(got_ref))


def unpack(keep, got, scalars, shape, earlier):
    count, units = keep.shape[:2]
    planes, points = shape[1], shape[3]
    spec = pl.BlockSpec((1,) + keep.shape[1:], lambda i, k, s: (i, 0, 0, 0, 0, 0))
    held = [] if earlier is None else [earlier]
    return pl.pallas_call(
        unpack_body,
        grid_spec=pltpu.PrefetchScalarGridSpec(
            num_scalar_prefetch=1,
            grid=(count, 2),
            in_specs=[spec, spec] + [pl.BlockSpec(memory_space=pl.ANY) for _ in held],
            out_specs=pl.BlockSpec(
                (1, planes, 2 * STEP * units, points), lambda i, k, s: (s[i], 0, s[count + k], 0)
            ),
        ),
        out_shape=jax.ShapeDtypeStruct(shape, jnp.float32),
        input_output_aliases={3: 0} if held else {},
        compiler_params=pltpu.CompilerParams(vmem_limit_bytes=VMEM_LIMIT),
        name="unpack",
    )(scalars, keep, got, *held)


def orbital_parts(same, first, second):
    pieces = range(first.shape[0])
    near = [jnp.where(same, first[d, 0], second[d, 0]) for d in pieces]
    far = [jnp.where(same, second[d, 0], first[d, 0]) for d in pieces]
    return near + far


def forward_body(scalars, near, far, first, second, lower_ref, upper_ref, planes_ref, keep_out, give_out):
    orbitals = orbital_parts(scalars[0] == 1, first, second)
    targets = [part[d, 0] for part in (near, far) for d in range(part.shape[0])]
    density = jnp.concatenate([t * o for t, o in zip(targets, orbitals)], axis=2)
    step, points = density.shape[1], density.shape[2]
    matrix = halves(planes_ref[...])
    results = []
    for part, weights in ((0, lower_ref), (1, upper_ref)):
        packed = jnp.concatenate([density[part], density[2]], axis=-1).reshape(step * points, 2 * LANES)
        lines = multiply_deep(halves(packed), halves(weights[...]))
        high, low = halves(lines)
        for row in range(step):
            where = slice(row * points, (row + 1) * points)
            results.append(multiply_deep(matrix, (high[where], low[where])))
    spectrum = jnp.swapaxes(jnp.stack(results), 0, 1)
    keep_out[...] = spectrum[: points // 2]
    give_out[...] = spectrum[points // 2 :]


def stacked(array, offset, layers):
    return pl.BlockSpec((layers, 1) + array.shape[2:], lambda u, s: (0, u + offset, 0, 0, 0, 0))


def forward(near, far, first, at, second, there, scalars, lower, upper, planes_matrix):
    units, points = near.shape[1], planes_matrix.shape[0]
    whole = lambda a: pl.BlockSpec(a.shape, lambda u, s: (0, 0))
    out = pl.BlockSpec((points // 2, 2 * STEP, points), lambda u, s: (0, u, 0))
    shape = jax.ShapeDtypeStruct((points // 2, 2 * STEP * units, points), jnp.float32)
    return pl.pallas_call(
        forward_body,
        grid_spec=pltpu.PrefetchScalarGridSpec(
            num_scalar_prefetch=1,
            grid=(units,),
            in_specs=[stacked(a, at, near.shape[0]) for a, at in ((near, 0), (far, 0), (first, at), (second, there))]
            + [whole(lower), whole(upper), whole(planes_matrix)],
            out_specs=[out, out],
        ),
        out_shape=[shape, shape],
        compiler_params=pltpu.CompilerParams(vmem_limit_bytes=VMEM_LIMIT),
        name="forward",
    )(scalars, near, far, first, second, lower, upper, planes_matrix)


def middle_body(count, kernel_ref, forth_ref, back_ref, *refs):
    ins, outs = refs[:count], refs[count:]
    forth, back = halves(forth_ref[...]), halves(back_ref[...])
    for k in range(kernel_ref.shape[0]):
        rows = jnp.concatenate([r[k] for r in ins], axis=0)
        half, tail = rows.shape[0] // 2, rows.shape[1] - LANES
        top = kernel_ref[k, :half]
        first_row = lax.broadcasted_iota(jnp.int32, top.shape, 0) == 0
        table = jnp.concatenate([top, jnp.where(first_row, kernel_ref[k, half : half + 1], top)], axis=0)
        table = jnp.concatenate([table, table[:, :tail]], axis=1)
        spectrum = multiply(forth, halves(rows)) * table
        filtered = multiply(back, halves(spectrum))
        start = 0
        for out in outs:
            out[k] = filtered[start : start + out.shape[1]]
            start += out.shape[1]


def middle(spectra, kernel, forth, back):
    count = len(spectra)
    deep, _, points = spectra[0].shape
    block = 16
    parts = [pl.BlockSpec((block,) + a.shape[1:], lambda k: (k, 0, 0)) for a in spectra]
    whole = pl.BlockSpec((points, points), lambda k: (0, 0))
    return pl.pallas_call(
        lambda *refs: middle_body(count, *refs),
        grid=(deep // block,),
        in_specs=[pl.BlockSpec((block,) + kernel.shape[1:], lambda k: (k, 0, 0)), whole, whole] + parts,
        out_specs=parts,
        out_shape=[jax.ShapeDtypeStruct(a.shape, jnp.float32) for a in spectra],
        compiler_params=pltpu.CompilerParams(vmem_limit_bytes=VMEM_LIMIT),
        name="middle",
    )(kernel, forth, back, *spectra)


def inverse_body(scalars, keep_ref, got_ref, first, second, lower_ref, upper_ref, planes_ref, near, far):
    spectrum = jnp.swapaxes(jnp.concatenate([keep_ref[...], got_ref[...]], axis=0), 0, 1)
    points = spectrum.shape[1]
    step = spectrum.shape[0] // 2
    matrix = halves(planes_ref[...])
    packed = []
    for part, weights in ((0, lower_ref), (1, upper_ref)):
        lines = jnp.concatenate(
            [multiply(matrix, halves(spectrum[part * step + row])) for row in range(step)], axis=0
        )
        packed.append(multiply(halves(lines), halves(weights[...])).reshape(step, points, 2 * LANES))
    low, high = packed
    field = [low[:, :, :LANES], high[:, :, :LANES], low[:, :, LANES:] + high[:, :, LANES:]]
    orbitals = orbital_parts(scalars[0] == 1, first, second)
    outs = [(part, d) for part in (near, far) for d in range(part.shape[0])]
    planes = points // len(outs)
    for i, (orbital, (out, d)) in enumerate(zip(orbitals, outs)):
        for part in range(3):
            out[d, 0, part] = -field[part][:, i * planes : (i + 1) * planes] * orbital[part]


def inverse(keep, got, skip, units, first, at, second, there, scalars, lower, upper, planes_matrix):
    deep, _, points = keep.shape
    whole = lambda a: pl.BlockSpec(a.shape, lambda u, s: (0, 0))
    part = pl.BlockSpec((deep, 2 * STEP, points), lambda u, s: (0, u + skip, 0))
    layers = first.shape[0]
    shape = jax.ShapeDtypeStruct((layers, units) + first.shape[2:], jnp.float32)
    return pl.pallas_call(
        inverse_body,
        grid_spec=pltpu.PrefetchScalarGridSpec(
            num_scalar_prefetch=1,
            grid=(units,),
            in_specs=[part, part, stacked(first, at, layers), stacked(second, there, layers)]
            + [whole(lower), whole(upper), whole(planes_matrix)],
            out_specs=[stacked(shape, 0, layers)] * 2,
        ),
        out_shape=[shape] * 2,
        compiler_params=pltpu.CompilerParams(vmem_limit_bytes=VMEM_LIMIT),
        name="inverse",
    )(scalars, keep, got, first, second, lower, upper, planes_matrix)


def by_layers(bands, occupied, occ_index, band_pick, groups, slabs):
    picks, window = band_pick.shape[0], occ_index.shape[0]
    per_group, planes, points = occupied.shape[0], bands.shape[1], bands.shape[2]
    sides = window
    layers = slabs // sides
    half_rows = points // CORES
    units = half_rows // (2 * STEP)
    chunks = len(SPLIT)
    starts = [sum(SPLIT[:j]) for j in range(chunks)]

    band, slab = lax.axis_index("band"), lax.axis_index("slab")
    y, c = band // CORES, band % CORES
    z, x = slab // sides, slab % sides

    def swap(values, axis, size, flip):
        return lax.ppermute(values, axis, [(i, flip(i)) for i in range(size)])

    def over_core(values):
        return swap(values, "band", groups, lambda i: i ^ 1)

    def over_y(values):
        return swap(values, "band", groups, lambda i: i ^ CORES)

    def over_x(values):
        return swap(values, "slab", slabs, lambda i: i ^ 1)

    def over_z(values, d):
        return swap(values, "slab", slabs, lambda i: i ^ (d * sides))

    layer_of = z ^ jnp.arange(layers, dtype=jnp.int32)
    side_of = x ^ jnp.arange(sides, dtype=jnp.int32)
    slab_of = (side_of[:, None] + sides * layer_of[None, :]).reshape(-1)
    plane_of = (slab_of[:, None] * planes + jnp.arange(planes, dtype=jnp.int32)).reshape(-1)
    core_of = c ^ jnp.arange(CORES, dtype=jnp.int32)
    all_modes = jnp.arange(points, dtype=jnp.int32)
    mode_of = (core_of[:, None] * half_rows + jnp.arange(half_rows, dtype=jnp.int32)).reshape(-1)

    tail = points - LANES
    low = jnp.arange(half_rows, dtype=jnp.int32)
    row_modes = jnp.concatenate([low, jnp.where(low == 0, half_rows, points - low)])
    near_columns = jnp.arange(tail, dtype=jnp.int32) + 1
    rest = jnp.arange(LANES - tail, dtype=jnp.int32)
    column_modes = jnp.concatenate([near_columns, jnp.where(rest == 0, 0, rest + tail), points - near_columns])
    row_squares = wave_squared(jnp.arange(half_rows + 2 * STEP, dtype=jnp.int32), points)
    column_squares = wave_squared(column_modes[:LANES], points)
    own_squares = wave_squared(c * half_rows + jnp.arange(half_rows, dtype=jnp.int32), points)

    first_bit = z % picks
    target_index = band_pick[jnp.arange(picks, dtype=jnp.int32) ^ first_bit]
    which = occ_index[side_of]
    owner = which // per_group
    owner_y, owner_core = owner // CORES, owner % CORES
    here = z // picks == c
    same = x == y
    flag = same.astype(jnp.int32)[None]

    def row_blocks(start, size):
        return jnp.stack([c * (units // size) + start // size, (1 - c) * (units // size) + start // size])

    def sync(*values):
        return lax.optimization_barrier(values)

    def after(value, *others):
        return lax.optimization_barrier((value,) + others)[0]

    def pack_orbital(h, parts, *earlier):
        start, size = starts[PARTS[h][0]], sum(SPLIT[j] for j in PARTS[h])
        scalars = jnp.concatenate([which % per_group, row_blocks(start, size)])
        return pack(occupied, after(scalars, *earlier), size, parts)

    def pack_target(j, parts, *earlier):
        scalars = jnp.concatenate([target_index, row_blocks(starts[j], SPLIT[j])])
        return pack(bands, after(scalars, *earlier), SPLIT[j], parts)


    def choose_orbital(keep, got):
        mine = jnp.where(owner_core[0] == c, keep[0], got[0])
        theirs = jnp.where(owner_core[1] == c, keep[1], got[1])
        return mine, theirs

    def choose_side(mine, other):
        return jnp.where(same, mine, other), jnp.where(same, other, mine)

    def choose_group(stay, got):
        return jnp.where(owner_y[0] == y, stay, got)

    def choose_targets(j, keep, got, carried=None):
        pieces = []
        begin = starts[j] - (starts[1] if j else 0)
        for d in range(layers):
            a, b = (keep, got) if d < picks else (got, keep)
            piece = jnp.where(here, a[d % picks], b[d % picks])[begin : begin + SPLIT[j]]
            if carried is not None and d and not d & (d - 1):
                piece = jnp.concatenate([piece, carried], axis=0)
            pieces.append(piece)
        return pieces

    def along_layers(pieces, carried=None):
        got, reached, size = [], [carried], pieces[0].shape[0]
        for d, piece in enumerate(pieces):
            moved = over_z(piece, d) if d else piece
            got.append(moved[:size])
            if carried is not None and d:
                reach = d & -d
                reached.append(over_z(reached[d - reach], reach) if d & (d - 1) else moved[size:])
        return got, reached

    size = SPLIT[0]
    keep, give = pack_target(0, 1)
    got = over_core(give)
    ready = choose_targets(0, keep, got)
    ready = sync(ready)[0]
    near0, _ = along_layers(ready)
    keep, give = pack_orbital(0, 1, ready)
    got = over_core(give)
    mine, theirs = choose_orbital(keep, got)
    other = over_x(theirs)
    stay, send = choose_side(mine, other)
    carried0 = choose_group(stay, over_y(send))
    keep, give = pack_orbital(1, 2, keep)
    mine, theirs = choose_orbital(keep, over_core(give))
    stay, send = choose_side(mine, over_x(theirs))
    keep, give = pack_target(1, chunks - 1, keep)
    got = over_core(give)
    ready = choose_targets(1, keep, got, carried0)
    ready, carried0, near0, stay, send, keep, got = sync(ready, carried0, near0, stay, send, keep, got)
    near1, first0 = along_layers(ready, carried0)
    near0 = jnp.stack(near0)
    far0 = over_x(near0)
    carried = choose_group(stay, over_y(send))
    carried1, carried2 = carried[:size], carried[size:]
    ready = choose_targets(2, keep, got, carried1)
    ready, carried1, carried2, near1, first0, far0 = sync(ready, carried1, carried2, near1, first0, far0)
    near2, first1 = along_layers(ready, carried1)
    first0, near1 = jnp.stack(first0), jnp.stack(near1)
    second0 = over_y(first0)
    far1 = over_x(near1)
    ready = choose_targets(3, keep, got, carried2)
    own_squares, row_squares, column_squares, all_modes, row_modes, column_modes, mode_of, plane_of = after(
        (own_squares, row_squares, column_squares, all_modes, row_modes, column_modes, mode_of, plane_of), near2[1]
    )
    kernel = screened(own_squares[:, None, None] + row_squares[None, :, None] + column_squares[None, None, :])
    kernel = kernel / float(points * points * points)
    columns = cas_matrix(all_modes, column_modes, points)
    columns_back = cas_matrix(column_modes, all_modes, points)
    empty = jnp.zeros((points - LANES, points), jnp.float32)
    lower = jnp.concatenate([columns, empty], axis=0)
    upper = jnp.concatenate([columns[:LANES], empty, columns[LANES:]], axis=0)
    lower_back = jnp.concatenate([columns_back, empty.T], axis=1)
    upper_back = jnp.concatenate([columns_back[:, :LANES], empty.T, columns_back[:, LANES:]], axis=1)
    to_modes = cas_matrix(mode_of, plane_of, points)
    to_planes = cas_matrix(plane_of, mode_of, points)
    forth = cas_matrix(row_modes, mode_of, points)
    back = cas_matrix(mode_of, row_modes, points)
    matrices = lower, upper, lower_back, upper_back, to_modes, to_planes, forth, back
    ready, carried2, near2, first1, far1, second0, kernel, matrices = sync(
        ready, carried2, near2, first1, far1, second0, kernel, matrices
    )
    lower, upper, lower_back, upper_back, to_modes, to_planes, forth, back = matrices
    near3, first2 = along_layers(ready, carried2)
    first1, near2 = jnp.stack(first1), jnp.stack(near2)
    second1 = over_y(first1)
    far2 = over_x(near2)
    ready = choose_targets(4, keep, got)
    keep0, give0 = forward(near0, far0, first0, 0, second0, 0, flag, lower, upper, to_modes)
    ready, near3, first2, second1, far2, keep0, give0 = sync(ready, near3, first2, second1, far2, keep0, give0)
    near4, _ = along_layers(ready)
    split = SPLIT[PARTS[2][0]]
    first3 = jnp.stack([piece[split:] for piece in first2])
    first2, near3 = jnp.stack([piece[:split] for piece in first2]), jnp.stack(near3)
    second2 = over_y(first2)
    far3 = over_x(near3)
    got0 = over_core(give0)
    keep1, give1 = forward(near1, far1, first1, 0, second1, 0, flag, lower, upper, to_modes)
    near4, far3, second2, first3, got0, keep1, give1 = sync(near4, far3, second2, first3, got0, keep1, give1)
    cut = SPLIT[4] // 2
    near4 = [jnp.stack([piece[at : at + cut] for piece in near4]) for at in (0, cut)]
    far4 = [over_x(near4[0])]
    far4.append(over_x(near4[1]))
    second3 = over_y(first3)
    got1 = over_core(give1)
    keep2, give2 = forward(near2, far2, first1, SPLIT[1], second1, SPLIT[1], flag, lower, upper, to_modes)
    got2 = over_core(give2)
    keep3, give3 = forward(near3, far3, first2, 0, second2, 0, flag, lower, upper, to_modes)
    got3 = over_core(give3)
    keep4, give4 = forward(near4[0], far4[0], first3, 0, second3, 0, flag, lower, upper, to_modes)
    got4 = over_core(give4)
    keep5, give5 = forward(near4[1], far4[1], first3, cut, second3, cut, flag, lower, upper, to_modes)
    got5 = over_core(give5)

    spectra = [keep0, keep1, keep2, keep3, keep4, keep5, got0, got1, got2, got3, got4, got5]
    filtered = middle(spectra, kernel, forth, back)

    orbit = [
        (first0, 0, second0, 0),
        (first1, 0, second1, 0),
        (first1, SPLIT[1], second1, SPLIT[1]),
        (first2, 0, second2, 0),
        (first3, 0, second3, 0),
    ]
    back_got = [over_core(values) for values in filtered[chunks + 1 :]]
    queue = [(j, skip, BACK) for j in range(chunks - 1) for skip in range(0, SPLIT[j], BACK)]
    queue = [(chunks, 0, cut), (chunks - 1, 0, cut)] + queue[::-1]
    orbit.append((first3, cut, second3, cut))
    starts.append(starts[-1] + cut)
    result, home, sums = None, None, None
    for turn in range(len(queue) + 2):
        near = far = got = pieces = None
        if turn < len(queue):
            j, skip, count = queue[turn]
            first, at, second, there = orbit[j]
            orbitals = first, at + skip, second, there + skip
            near, far = inverse(
                filtered[j], back_got[j], skip, count, *orbitals, flag, lower_back, upper_back, to_planes
            )
        if turn:
            near, far, sums, home, result = sync(near, far, sums, home, result)
        if far is not None:
            got = over_x(far)
        if sums is not None:
            pieces = [sums[0][d] + sums[1][d] for d in range(layers)]
            pieces = [over_z(piece, d) if d else piece for d, piece in enumerate(pieces)]
        if home is not None:
            j, skip, count = queue[turn - 2]
            kept, sent = jnp.stack(home[:picks]), jnp.stack(home[picks:])
            own = jnp.where(here, kept, sent)
            other = over_core(jnp.where(here, sent, kept))
            index = jnp.arange(picks, dtype=jnp.int32) ^ first_bit
            place = jnp.concatenate([index, row_blocks(starts[j] + skip, count)])
            result = unpack(own, other, place, (picks,) + bands.shape[1:], result)
        sums = None if far is None else (near, got)
        home = pieces
    return result


def broadcast(x, axis, root):
    mine = lax.axis_index(axis) == root
    return lax.psum(jnp.where(mine, x, jnp.zeros_like(x)), axis)


def by_lines(bands, occupied, occ_index, band_pick):
    points, planes = bands.shape[2], bands.shape[1]
    window, per_group = occ_index.shape[0], occupied.shape[0]
    modes = jnp.arange(points, dtype=jnp.int32)
    matrix = cas_matrix(modes, modes, points)
    squares = wave_squared(modes, points)

    def transform(pattern, values):
        return jnp.einsum(pattern, values, matrix, precision=lax.Precision.HIGHEST)

    along_z, along_y, along_x = "pxyz,zk->pxyk", "pxyz,yk->pxkz", "pxyz,xk->pkyz"
    offset = lax.axis_index("slab") * planes
    row_squares = lax.dynamic_slice_in_dim(squares, offset, planes)
    kernel = screened(squares[:, None, None] + row_squares[None, :, None] + squares[None, None, :])
    kernel = kernel / float(points * points * points)
    targets = jnp.take(bands, band_pick, axis=0)

    def fetch_orbital(turn):
        which = occ_index[turn]
        own_orbital = lax.dynamic_index_in_dim(occupied, which % per_group, 0, keepdims=False)
        return broadcast(own_orbital, "band", which // per_group)

    orbitals = lax.map(fetch_orbital, jnp.arange(window, dtype=jnp.int32))
    density = (orbitals[:, None] * targets[None]).reshape((-1,) + targets.shape[1:])
    lines = transform(along_y, transform(along_z, density))
    lines = lax.all_to_all(lines, "slab", split_axis=2, concat_axis=1, tiled=True)
    lines = transform(along_x, kernel[None] * transform(along_x, lines))
    lines = lax.all_to_all(lines, "slab", split_axis=1, concat_axis=2, tiled=True)
    field = transform(along_z, transform(along_y, lines)).reshape((window,) + targets.shape)
    return -jnp.sum(field * orbitals[:, None], axis=0)


def solution(mesh):
    groups, slabs = mesh.shape["band"], mesh.shape["slab"]

    def shards(bands, occupied, occ_index, band_pick):
        picks, window = band_pick.shape[0], occ_index.shape[0]
        planes, points = bands.shape[1], bands.shape[2]
        fits = (
            window == 2
            and picks == 2
            and bands.shape[0] == picks
            and groups == 2 * CORES
            and slabs == CORES * picks * window
            and planes % 8 == 0
            and 2 * (points - LANES) == LANES
            and points == CORES * 2 * STEP * sum(SPLIT)
        )
        if fits:
            return by_layers(bands, occupied, occ_index, band_pick, groups, slabs)
        return by_lines(bands, occupied, occ_index, band_pick)

    placed = (P("band", "slab", None, None), P("band", "slab", None, None), P(), P("band"))
    return jax.shard_map(
        shards, mesh=mesh, in_specs=placed, out_specs=P("band", "slab", None, None), check_vma=False
    )
```
